256 devices in a mesh: tm: 8 (over y, core), lon: 16 (over x_hi, z), head: 2 (over x_lo).
Axes of the slice: x: 4 (x_hi: 2, x_lo: 2; x = x_hi * 2 + x_lo), y: 4, z: 8, core: 2. Of those that a mesh axis runs over, the one named last changes fastest.
Arguments:
- query_field: bfloat16 [96, 8, 128, 1536], P('tm', None, 'lon', 'head'), may hold values from -8 to 8
- key_field: bfloat16 [96, 8, 128, 1536], P('tm', None, 'lon', 'head'), may hold values from -8 to 8
- value_field: bfloat16 [96, 8, 128, 1536], P('tm', None, 'lon', 'head'), may hold values from -6 to 6
- tile_offsets: int32 [16, 16], P('tm', 'lon'), may hold values from -1 to 1
- timesteps: int32 [16], P('tm'), may hold values from 0 to 999
- gate_weight: float32 [256, 1536], P(None, 'head'), may hold values from -0.375 to 0.375
Outputs:
- gated_field: bfloat16 [96, 8, 128, 1536], P('tm', None, 'lon', 'head')
The draws below stay inside these ranges and needn't reach their ends.
Inputs may be any that keep to these rules, and one draw needn't show every extreme that they name: `tile_offsets`: the query tile (t, L) with shift s attends longitude tiles L + s - 1 to L + s + 1 around the loop.
All inputs are finite; a program needn't handle non-finite values.
Results may differ from the reference program's by a relative error of at most 0.0037.
Values may be sent and summed in bfloat16 or wider, within the bound.
No kernel may reach another device: no remote copies, remote signals or barrier semaphores. Data moves between devices by JAX's collectives and lax.ppermute only.
A program may use at most 128 MiB of HBM per device.

```python
import math
import jax
import jax.numpy as jnp
from jax import lax

HEADS = 12
HD = 128
FREQ = 256
TILE_T = 6
TILE_H = 8
TILE_W = 8
NTT = 16
FRAMES = 96
COLS = 128
F = 1536
N_LON = 16


def draw_query_field(key, part):
    key = jax.random.fold_in(key, 11)
    base_key = jax.random.fold_in(key, 0)
    full_shape = (FRAMES, TILE_H, COLS, HEADS, HD)
    drawn = jnp.clip(jax.random.normal(base_key, full_shape, jnp.float32), -8.0, 8.0)
    return drawn.reshape(FRAMES, TILE_H, COLS, HEADS * HD).astype(jnp.bfloat16)


def draw_key_field(key, part):
    key = jax.random.fold_in(key, 23)
    base_key = jax.random.fold_in(key, 0)
    full_shape = (FRAMES, TILE_H, COLS, HEADS, HD)
    drawn = jnp.clip(2.0 * jax.random.normal(base_key, full_shape, jnp.float32), -8.0, 8.0)
    return drawn.reshape(FRAMES, TILE_H, COLS, HEADS * HD).astype(jnp.bfloat16)


def set_ends(result, rng, low, largest):
    extent = result.shape
    index_at = [jax.random.randint(jax.random.fold_in(rng, axis), (), 0, extent[axis]) for axis in range(len(extent))]
    result = result.at[tuple(index_at)].set(low)
    longest = extent.index(max(extent))
    index_at[longest] = (index_at[longest] + 1) % extent[longest]
    return result.at[tuple(index_at)].set(largest)


def block_scale(own_key, shape, cuts, low, largest):
    def one(position, blocks):
        draws = jax.random.uniform(jax.random.fold_in(jax.random.fold_in(own_key, 6), position), (blocks,), jnp.float32, low / len(cuts), largest / len(cuts))
        return jnp.repeat(jnp.exp(draws), shape[position] // blocks).reshape((-1,) + (1,) * (len(shape) - position - 1))

    loudness = one(*cuts[0])
    for cut in cuts[1:]:
        loudness = loudness * one(*cut)
    return loudness


def noise(own_key, shape, deviation, bound, cuts=(), kind=jnp.bfloat16):
    gain = block_scale(own_key, shape, cuts, -0.22, 0.18) if cuts else 1.0
    result = jax.random.normal(own_key, shape, jnp.float32) * deviation * gain
    return jnp.minimum(jnp.maximum(result, -bound), bound).astype(kind)


def setup_inputs(seed: int = 0) -> dict:
    key_of = jax.random.split(jax.random.key(seed), 7)
    query_field = draw_query_field(jax.random.fold_in(key_of[6], 71), 0)
    key_field = draw_key_field(jax.random.fold_in(key_of[6], 71), 0)
    value_field = noise(key_of[2], (FRAMES, TILE_H, COLS, F), 1.0, 6.0, ((0, 8), (2, 16), (3, 2)))
    tile_offsets = set_ends(jax.random.randint(key_of[3], (NTT, N_LON), -1, 2), jax.random.fold_in(key_of[3], 1), -1, 1).astype(jnp.int32)
    timesteps = set_ends(jax.random.randint(key_of[4], (NTT,), 0, 1000), jax.random.fold_in(key_of[4], 1), 0, 999).astype(jnp.int32)
    gate_weight = noise(key_of[5], (FREQ, F), FREQ ** -0.5, 0.375, ((1, 2),), jnp.float32)
    return dict(query_field=query_field, key_field=key_field, value_field=value_field, tile_offsets=tile_offsets, timesteps=timesteps, gate_weight=gate_weight)


def start_at(*entries):
    return tuple((jnp.asarray(entry).astype(jnp.int32) for entry in entries))

def reference(query_field, key_field, value_field, tile_offsets, timesteps, gate_weight):
    half_freq = FREQ // 2
    frequencies = jnp.exp(-math.log(10000.0) * jnp.arange(half_freq, dtype=jnp.float32) / half_freq)
    angles = timesteps.astype(jnp.float32)[:, None] * frequencies[None, :]
    embedding = jnp.concatenate([jnp.cos(angles), jnp.sin(angles)], axis=1)
    gate_rows = jnp.dot(embedding, gate_weight, precision=lax.Precision.HIGHEST, preferred_element_type=jnp.float32)
    lon_count = COLS // TILE_W
    tile_size = TILE_T * TILE_H * TILE_W
    keys_padded = jnp.pad(key_field, ((TILE_T, TILE_T), (0, 0), (0, 0), (0, 0)))
    values_padded = jnp.pad(value_field, ((TILE_T, TILE_T), (0, 0), (0, 0), (0, 0)))
    inv_root = 1.0 / math.sqrt(HD)

    def one_tile(tile_index):
        time_tile = (tile_index // lon_count).astype(jnp.int32)
        lon_tile = (tile_index % lon_count).astype(jnp.int32)
        lon_shift = tile_offsets[time_tile, lon_tile].astype(jnp.int32)
        query_rows = lax.dynamic_slice(query_field, start_at(time_tile * TILE_T, 0, lon_tile * TILE_W, 0), (TILE_T, TILE_H, TILE_W, F))
        query_rows = query_rows.reshape(tile_size, HEADS, HD).astype(jnp.float32)
        col_index = jnp.mod((lon_tile + lon_shift - 1) * TILE_W + jnp.arange(3 * TILE_W, dtype=jnp.int32), COLS).astype(jnp.int32)
        key_block = lax.dynamic_slice(keys_padded, start_at(time_tile * TILE_T, 0, 0, 0), (3 * TILE_T, TILE_H, COLS, F))
        value_block = lax.dynamic_slice(values_padded, start_at(time_tile * TILE_T, 0, 0, 0), (3 * TILE_T, TILE_H, COLS, F))
        key_block = jnp.take(key_block, col_index, axis=2).reshape(3, TILE_T * TILE_H * 3 * TILE_W, HEADS, HD).astype(jnp.float32)
        value_block = jnp.take(value_block, col_index, axis=2).reshape(3, TILE_T * TILE_H * 3 * TILE_W, HEADS, HD).astype(jnp.float32)
        window_times = time_tile - 1 + jnp.arange(3, dtype=jnp.int32)
        usable = (window_times >= 0) & (window_times < NTT)
        scores = jnp.einsum('qhd,jkhd->hqjk', query_rows, key_block) * inv_root
        scores = jnp.where(usable[None, None, :, None], scores, -1e+30)
        row_max = lax.optimization_barrier(jnp.max(scores, axis=(2, 3), keepdims=True))
        raised = jnp.exp(scores - row_max)
        totals = lax.optimization_barrier(jnp.sum(raised, axis=(2, 3)))
        weights = raised.astype(jnp.bfloat16)
        weighted = jnp.einsum('hqjk,jkhd->qhd', weights.astype(jnp.float32), value_block)
        gated = weighted / jnp.transpose(totals)[:, :, None] * gate_rows[time_tile].reshape(HEADS, HD)[None, :, :]
        return gated.astype(jnp.bfloat16)
    results = lax.map(one_tile, jnp.arange(NTT * lon_count, dtype=jnp.int32))
    results = results.reshape(NTT, lon_count, TILE_T, TILE_H, TILE_W, F)
    results = jnp.transpose(results, (0, 2, 3, 1, 4, 5))
    return results.reshape(FRAMES, TILE_H, COLS, F)
```

```python
import functools
import itertools
import math

import jax
import jax.numpy as jnp
from jax import lax
from jax.experimental import pallas as pl
from jax.experimental.pallas import tpu as pltpu
from jax.sharding import PartitionSpec as P

HD = 128
FREQ = 256
ROWS = 384
TT = 6
SCALE = math.log2(math.e) / math.sqrt(HD)
GROUPS = ((0, 3), (3, 2), (5, 1))
ANY = pl.BlockSpec(memory_space=pltpu.HBM)
SMALL = pl.CostEstimate(flops=0, bytes_accessed=1024, transcendentals=0)
VMEM = pl.BlockSpec(memory_space=pltpu.VMEM)
SMEM = pl.BlockSpec(memory_space=pltpu.SMEM)


def run_copies(copies):
    for copy in copies:
        copy.start()
    for copy in copies:
        copy.wait()


def split_kernel(groups, k_ref, v_ref, *refs):
    outs, sem = refs[:-1], refs[-1]
    copies = []
    for out, (first, count) in zip(outs, groups):
        for t in range(2):
            for i in range(count):
                for which, ref in enumerate((k_ref, v_ref)):
                    lanes = pl.ds((first + i) * HD, HD)
                    copies.append(pltpu.make_async_copy(ref.at[pl.ds(t * TT, TT), :, :, lanes], out.at[i, t, which], sem.at[len(copies)]))
    run_copies(copies)


def split(k, v, groups):
    outs = pl.pallas_call(
        functools.partial(split_kernel, groups),
        out_shape=[jax.ShapeDtypeStruct((n, 2, 2, TT, 8, 8, HD), k.dtype) for _, n in groups],
        in_specs=[ANY, ANY],
        out_specs=[VMEM] * len(groups),
        scratch_shapes=[pltpu.SemaphoreType.DMA((4 * sum(n for _, n in groups),))],
        cost_estimate=SMALL,
        compiler_params=pltpu.CompilerParams(vmem_limit_bytes=60 * 2**20),
        name=f"split_{groups[0][0]}",
    )(k, v)
    return [x.reshape(x.shape[:3] + (ROWS, HD)) for x in outs]


def pack_kernel(rows, place_ref, *refs):
    ins, (off, on, sem) = refs[:-3], refs[-3:]
    core = place_ref[0]
    copies = []
    for ref, (row, start, count) in zip(ins, rows):
        for out, tile in ((off, core), (on, 1 - core)):
            copies.append(pltpu.make_async_copy(ref.at[:, tile], out.at[row, pl.ds(start, count)], sem.at[len(copies)]))
    run_copies(copies)


def pack(name, place, *sides):
    rows = []
    for row, xs in enumerate(sides):
        start = 0
        for x in xs:
            rows.append((row, start, x.shape[0]))
            start += x.shape[0]
    shape = jax.ShapeDtypeStruct((len(sides), start) + xs[0].shape[2:], xs[0].dtype)
    return pl.pallas_call(
        functools.partial(pack_kernel, rows),
        out_shape=[shape, shape],
        in_specs=[SMEM] + [ANY] * len(rows),
        out_specs=[VMEM, VMEM],
        scratch_shapes=[pltpu.SemaphoreType.DMA((2 * len(rows),))],
        cost_estimate=SMALL,
        compiler_params=pltpu.CompilerParams(vmem_limit_bytes=60 * 2**20),
        name=name,
    )(place, *[x for xs in sides for x in xs])


def attn_kernel(plan, first, count, s_ref, place_ref, q_ref, *refs):
    names, starts, finishes, sides, pick = plan
    ops = dict(zip(names, refs))
    out_ref, kv, qv, sc0, sc1, top0, top1, si, so, ov, ksem, qsem, isem, osem = refs[len(refs) - 14:]
    core, cut = place_ref[0], place_ref[1]

    def fill(i, slot):
        h = first + i
        for t in range(2):
            side = pick(s_ref[t, 0])
            for c, (segments, far, near) in enumerate(sides):
                for name, low, high in segments:
                    inside = (side == c) & (h >= low) & (h < high)

                    @pl.when(inside)
                    def _():
                        own = ops[name].at[h - low]
                        halo = kv.at[slot, t, 2 * t]
                        pltpu.make_async_copy(own, kv.at[slot, t, pl.ds(1 - t, 2)], ksem.at[slot, t]).start()
                        far_name, far_lead, far_low = far
                        near_name, near_lead, near_low = near
                        far_at = place_ref[2] if far_lead is None else far_lead

                        @pl.when((core == t) & (cut == 0))
                        def _():
                            pltpu.make_async_copy(ops[far_name].at[far_at, h - far_low], halo, ksem.at[slot, t]).start()

                        @pl.when((core == t) & (cut != 0))
                        def _():
                            pltpu.make_async_copy(own.at[t], halo, ksem.at[slot, t]).start()

                        @pl.when(core != t)
                        def _():
                            pltpu.make_async_copy(ops[near_name].at[near_lead, h - near_low], halo, ksem.at[slot, t]).start()
        q_copy(i, slot).start()
        if not starts:
            state_in(i, slot).start()

    def filled(i, slot):
        for t in range(2):
            pltpu.make_async_copy(kv.at[slot, t], kv.at[slot, t], ksem.at[slot, t]).wait()
        q_copy(i, slot).wait()
        if not starts:
            state_in(i, slot).wait()

    def lanes(i):
        return pl.ds(pl.multiple_of((first + i) * HD, HD), HD)

    def q_copy(i, slot):
        return pltpu.make_async_copy(q_ref.at[:, :, :, lanes(i)], qv.at[slot], qsem.at[slot])

    def state_in(i, slot):
        return pltpu.make_async_copy(ops["state"].at[first + i], si.at[slot], isem.at[slot])

    def result(i):
        slot = lax.rem(i, 2)
        if finishes:
            return pltpu.make_async_copy(ov.at[slot], out_ref.at[:, :, :, lanes(i)], osem.at[slot])
        return pltpu.make_async_copy(so.at[slot], out_ref.at[first + i], osem.at[slot])

    def scores(slot, t, sc, top):
        q = qv[slot, pl.ds(t * TT, TT)].reshape(ROWS, HD)
        m = None
        for j in range(3):
            s = lax.dot_general(q, kv[slot, t, j, 0], (((1,), (1,)), ((), ())), preferred_element_type=jnp.float32)
            sc[j] = s
            mj = jnp.maximum(jnp.maximum(s[:, :128], s[:, 128:256]), s[:, 256:])
            m = mj if m is None else jnp.maximum(m, mj)
            yield
        m = jnp.broadcast_to(jnp.max(m, axis=1, keepdims=True), (ROWS, HD))
        if not starts:
            m = jnp.maximum(m, si[slot, t, :, 2 * HD:])
        top[...] = m
        yield

    def weigh(i, slot, t, sc, top):
        to = lax.rem(i, 2)
        m1 = top[...]
        m = jnp.concatenate([m1] * 3, axis=1)
        acc = None
        if not starts:
            fade = jnp.exp2((si[slot, t, :, 2 * HD:] - m1) * SCALE)
            acc = si[slot, t, :, :2 * HD] * jnp.concatenate([fade, fade], axis=1)
        for j in range(3):
            p = jnp.exp2((sc[j] - m) * SCALE).astype(jnp.bfloat16)
            v2 = jnp.concatenate([kv[slot, t, j, 1], jnp.ones((ROWS, HD), jnp.bfloat16)], axis=1)
            if j == 2 * t:
                v2 = jnp.where((cut != 0) & (core == t), jnp.zeros_like(v2), v2)
            part = jnp.dot(p, v2, preferred_element_type=jnp.float32)
            acc = part if acc is None else acc + part
            yield
        if finishes:
            o = acc[:, :HD] / acc[:, HD:] * ops["gate"][t, first + i]
            ov[to, pl.ds(t * TT, TT)] = o.astype(jnp.bfloat16).reshape(TT, 8, 8, HD)
        else:
            so[to, t, :, :2 * HD] = acc
            so[to, t, :, 2 * HD:] = m1
        yield

    def both(*steps):
        for _ in itertools.zip_longest(*steps):
            pass

    def head(i, last):
        slot, ahead = lax.rem(i, 3), lax.rem(i + 1, 3)
        if not last:
            @pl.when(i + 2 < count)
            def _():
                fill(i + 2, lax.rem(i + 2, 3))

        @pl.when(i >= 2)
        def _():
            result(i - 2).wait()
        both(weigh(i, slot, 0, sc0, top0), scores(slot, 1, sc1, top1))
        if last:
            both(weigh(i, slot, 1, sc1, top1))
        else:
            filled(i + 1, ahead)
            both(weigh(i, slot, 1, sc1, top1), scores(ahead, 0, sc0, top0))
        result(i).start()

    fill(0, 0)
    if count > 1:
        fill(1, 1)
    filled(0, 0)
    both(scores(0, 0, sc0, top0))

    def step(i, _):
        head(i, False)
        return 0
    lax.fori_loop(0, count - 1, step, 0)
    head(jnp.int32(count - 1), True)
    for i in range(max(0, count - 2), count):
        result(i).wait()


PICKS = (lambda s: 0 * s, lambda s: jnp.where(s > 0, 1, 0), lambda s: jnp.where(s == 0, 2, jnp.where(s > 0, 1, 0)))


def attend(name, phase, first, count, *, s, place, q, arrays, sides, state=None, gate=None, prev=None):
    arrays = dict(arrays)
    if state is not None:
        arrays["state"] = state
    if gate is not None:
        arrays["gate"] = gate
    if prev is not None:
        arrays["prev"] = prev
    names = tuple(arrays)
    heads = q.shape[3] // HD
    plan = (names, phase == 0, phase == 2, sides, PICKS[phase])
    final = phase == 2
    shape = jax.ShapeDtypeStruct(q.shape, q.dtype) if final else jax.ShapeDtypeStruct((heads, 2, ROWS, 3 * HD), jnp.float32)
    aliases = {3 + names.index("prev"): 0} if prev is not None else {}
    return pl.pallas_call(
        functools.partial(attn_kernel, plan, first, count),
        out_shape=shape,
        in_specs=[SMEM, SMEM, ANY] + [VMEM if n == "gate" else ANY for n in names],
        out_specs=ANY,
        input_output_aliases=aliases,
        scratch_shapes=[
            pltpu.VMEM((3, 2, 3, 2, ROWS, HD), jnp.bfloat16),
            pltpu.VMEM((3, 12, 8, 8, HD), jnp.bfloat16),
            pltpu.VMEM((3, ROWS, ROWS), jnp.float32), pltpu.VMEM((3, ROWS, ROWS), jnp.float32),
            pltpu.VMEM((ROWS, HD), jnp.float32), pltpu.VMEM((ROWS, HD), jnp.float32),
            pltpu.VMEM((3, 2, ROWS, 3 * HD), jnp.float32),
            pltpu.VMEM((2, 2, ROWS, 3 * HD), jnp.float32),
            pltpu.VMEM((2, 12, 8, 8, HD), jnp.bfloat16),
            pltpu.SemaphoreType.DMA((3, 2)), pltpu.SemaphoreType.DMA((3,)),
            pltpu.SemaphoreType.DMA((3,)), pltpu.SemaphoreType.DMA((2,))],
        compiler_params=pltpu.CompilerParams(vmem_limit_bytes=60 * 2**20),
        cost_estimate=SMALL,
        name=name,
    )(s, place, q, *arrays.values())


def from_behind(block, distance):
    size = lax.axis_size("lon")
    return lax.ppermute(block, "lon", [((i - distance) % size, i) for i in range(size)])


def after(x, *others):
    return lax.optimization_barrier((x, *others))[0]


def pairs(off):
    size = lax.axis_size("tm")
    return [[i + off, (i + off + 1) % size] for i in range(0, size, 2)]


def far_gather(x):
    return lax.all_gather(x, "tm", axis_index_groups=pairs(1))


def far_swap(x):
    route = [r for a, b in pairs(1)[:-1] for r in ((a, b), (b, a))]
    return lax.ppermute(x, "tm", route)


def near_gather(x):
    return lax.all_gather(x, "tm", axis_index_groups=pairs(0))


def near_swap(x):
    route = [r for a, b in pairs(0) for r in ((a, b), (b, a))]
    return lax.ppermute(x, "tm", route)


def local(query_field, key_field, value_field, tile_offsets, timesteps, gate_weight):
    features = query_field.shape[3]
    heads = features // HD
    tiles = query_field.shape[0] // TT
    tm, size = lax.axis_index("tm"), lax.axis_size("tm")
    core = tm % 2
    other = jnp.where(tm == 0, 0, core)
    cut = ((tm == 0) | (tm == size - 1)).astype(jnp.int32)
    place = jnp.stack([core, cut, other]).astype(jnp.int32)

    xa, xb = split(key_field, value_field, ((0, 3), (3, 3)))
    ra1, la1 = from_behind(xa, 1), from_behind(xa, -1)
    rb1, lb1 = from_behind(xb, 1), from_behind(xb, -1)
    ra2, la2 = from_behind(ra1, 1), from_behind(la1, -1)
    rb2, lb2 = from_behind(rb1[:2], 1), from_behind(lb1[:2], -1)
    rc1, lc1 = lax.optimization_barrier((rb1[2:], lb1[2:], ra2, la2))[:2]
    rc2, lc2 = from_behind(rc1, 1), from_behind(lc1, -1)

    half_freq = FREQ // 2
    frequencies = jnp.exp(-math.log(10000.0) * jnp.arange(half_freq, dtype=jnp.float32) / half_freq)
    angles = timesteps.astype(jnp.float32)[:, None] * frequencies[None, :]
    embedding = jnp.concatenate([jnp.cos(angles), jnp.sin(angles)], axis=1)
    gate_rows = jnp.dot(
        embedding, gate_weight, precision=lax.Precision.HIGHEST, preferred_element_type=jnp.float32
    ).reshape(tiles, heads, HD)

    far, near = pack("pack0", place, [xa, xb])
    far0, near0 = far_gather(far).reshape((2,) + far.shape[1:]), near_swap(near)
    attn = functools.partial(attend, s=tile_offsets, place=place, q=query_field)
    arrays = dict(xa=xa, xb=xb, far0=far0, near0=near0)
    sides = [([("xa", 0, 3), ("xb", 3, 6)], ("far0", None, 0), ("near0", 0, 0))]
    state = attn("own", 0, 0, heads, arrays=arrays, sides=sides)

    pa, pb, qa, qb, state = lax.optimization_barrier((ra1, rb1, la1, lb1, state))
    far, near = pack("pack1", place, [pa, pb], [qa, qb])
    far1, near1 = far_swap(far), near_swap(near)
    arrays = dict(ra1=ra1, rb1=rb1, la1=la1, lb1=lb1, far1=far1, near1=near1)
    sides = [([("ra1", 0, 3), ("rb1", 3, 6)], ("far1", 0, 0), ("near1", 0, 0)),
             ([("la1", 0, 3), ("lb1", 3, 6)], ("far1", 1, 0), ("near1", 1, 0))]
    state = attn("next", 1, 0, heads, arrays=arrays, sides=sides, state=state)

    out = None
    for name, a, n, l1, r2, l2 in (("last_a", 0, 3, la1, ra2, la2), ("last_b", 3, 2, lb1, rb2, lb2), ("last_c", 5, 1, lb1, rc2, lc2)):
        if a == 3:
            r2, l2, state = lax.optimization_barrier((r2, l2, state))
        if a == 5:
            r2, l2, out = lax.optimization_barrier((r2, l2, out))
        far, near = pack("pack_" + name, place, [r2], [l2])
        arrays = dict(l1=l1, far1=far1, near1=near1, r2=r2, l2=l2, far2=far_swap(far), near2=near_swap(near))
        b = a - a % 3
        sides = [([("r2", a, a + n)], ("far2", 0, a), ("near2", 0, a)),
                 ([("l2", a, a + n)], ("far2", 1, a), ("near2", 1, a)),
                 ([("l1", b, b + 3)], ("far1", 1, 0), ("near1", 1, 0))]
        out = attn(name, 2, a, n, arrays=arrays, sides=sides, state=state, gate=gate_rows, prev=out)
    return out


def solution(mesh):
    return jax.shard_map(
        local,
        mesh=mesh,
        in_specs=(
            P("tm", None, "lon", "head"),
            P("tm", None, "lon", "head"),
            P("tm", None, "lon", "head"),
            P("tm", "lon"),
            P("tm"),
            P(None, "head"),
        ),
        out_specs=P("tm", None, "lon", "head"),
        check_vma=False,
    )
```

```python
import functools
import itertools
import math

import jax
import jax.numpy as jnp
from jax import lax
from jax.experimental import pallas as pl
from jax.experimental.pallas import tpu as pltpu
from jax.sharding import PartitionSpec as P

HD = 128
FREQ = 256
ROWS = 384
TT = 6
SCALE = math.log2(math.e) / math.sqrt(HD)
ANY = pl.BlockSpec(memory_space=pltpu.HBM)
SMALL = pl.CostEstimate(flops=0, bytes_accessed=1024, transcendentals=0)
VMEM = pl.BlockSpec(memory_space=pltpu.VMEM)
SMEM = pl.BlockSpec(memory_space=pltpu.SMEM)


PICKS = (lambda s: 0 * s, lambda s: jnp.where(s > 0, 1, 0), lambda s: jnp.where(s == 0, 2, jnp.where(s > 0, 1, 0)))


def run_copies(copies):
    for copy in copies:
        copy.start()
    for copy in copies:
        copy.wait()


def split_kernel(k_ref, v_ref, out, sem):
    copies = []
    for t in range(2):
        for i in range(out.shape[0]):
            for which, ref in enumerate((k_ref, v_ref)):
                source = ref.at[pl.ds(t * TT, TT), :, :, pl.ds(i * HD, HD)]
                copies.append(pltpu.make_async_copy(source, out.at[i, t, which], sem.at[len(copies)]))
    run_copies(copies)


def split(k, v):
    n = k.shape[3] // HD
    x = pl.pallas_call(
        split_kernel,
        out_shape=jax.ShapeDtypeStruct((n, 2, 2, TT, 8, 8, HD), k.dtype),
        in_specs=[ANY, ANY],
        out_specs=VMEM,
        scratch_shapes=[pltpu.SemaphoreType.DMA((4 * n,))],
        cost_estimate=SMALL,
        compiler_params=pltpu.CompilerParams(vmem_limit_bytes=60 * 2**20),
        name="split",
    )(k, v)
    return x.reshape(x.shape[:3] + (ROWS, HD))


def pack_kernel(cuts, pick, place_ref, *refs):
    n = len(refs) - 2 * len(cuts) - 1
    ins, far, near, sem = refs[:n], refs[n:n + len(cuts)], refs[n + len(cuts):-1], refs[-1]
    core = place_ref[0]
    for w, (outs, tile, side) in enumerate(((far, core, pick(place_ref[2])), (near, 1 - core, pick(place_ref[3])))):
        for c, ref in enumerate(ins):
            @pl.when(side == c)
            def _():
                for i, (out, (first, count)) in enumerate(zip(outs, cuts)):
                    pltpu.make_async_copy(ref.at[pl.ds(first, count), tile], out, sem.at[w, i]).start()
    for w, outs in enumerate((far, near)):
        for i, out in enumerate(outs):
            pltpu.make_async_copy(out, out, sem.at[w, i]).wait()


def pack(name, phase, place, xs, cuts):
    shapes = [jax.ShapeDtypeStruct((count,) + xs[0].shape[2:], xs[0].dtype) for _, count in cuts]
    outs = pl.pallas_call(
        functools.partial(pack_kernel, cuts, PICKS[phase]),
        out_shape=shapes + shapes,
        in_specs=[SMEM] + [ANY] * len(xs),
        out_specs=[VMEM] * (2 * len(cuts)),
        scratch_shapes=[pltpu.SemaphoreType.DMA((2, len(cuts)))],
        cost_estimate=SMALL,
        compiler_params=pltpu.CompilerParams(vmem_limit_bytes=60 * 2**20),
        name=name,
    )(place, *xs)
    return outs[:len(cuts)], outs[len(cuts):]


def attn_kernel(plan, first, count, s_ref, place_ref, q_ref, *refs):
    names, starts, finishes, sides, pick, halo_first = plan
    ops = dict(zip(names, refs))
    out_ref, kv, qv, sc0, sc1, top0, top1, si, so, ov, ksem, qsem, isem, osem = refs[len(refs) - 14:]
    core, cut = place_ref[0], place_ref[1]

    def fill(i, slot):
        h = first + i
        for t in range(2):
            side = pick(s_ref[t, 0])
            halo = kv.at[slot, t, 2 * t]
            for c, (name, low) in enumerate(sides):
                own = ops[name].at[h - low]

                @pl.when(side == c)
                def _():
                    pltpu.make_async_copy(own, kv.at[slot, t, pl.ds(1 - t, 2)], ksem.at[slot, t]).start()

                @pl.when((side == c) & (core == t) & (cut != 0))
                def _():
                    pltpu.make_async_copy(own.at[t], halo, ksem.at[slot, t]).start()

            @pl.when((core == t) & (cut == 0))
            def _():
                pltpu.make_async_copy(ops["far"].at[h - halo_first], halo, ksem.at[slot, t]).start()

            @pl.when(core != t)
            def _():
                pltpu.make_async_copy(ops["near"].at[h - halo_first], halo, ksem.at[slot, t]).start()
        q_copy(i, slot).start()
        if not starts:
            state_in(i, slot).start()

    def filled(i, slot):
        for t in range(2):
            pltpu.make_async_copy(kv.at[slot, t], kv.at[slot, t], ksem.at[slot, t]).wait()
        q_copy(i, slot).wait()
        if not starts:
            state_in(i, slot).wait()

    def lanes(i):
        return pl.ds(pl.multiple_of((first + i) * HD, HD), HD)

    def q_copy(i, slot):
        return pltpu.make_async_copy(q_ref.at[:, :, :, lanes(i)], qv.at[slot], qsem.at[slot])

    def state_in(i, slot):
        return pltpu.make_async_copy(ops["state"].at[first + i], si.at[slot], isem.at[slot])

    def result(i):
        slot = lax.rem(i, 2)
        if finishes:
            return pltpu.make_async_copy(ov.at[slot], out_ref.at[:, :, :, lanes(i)], osem.at[slot])
        return pltpu.make_async_copy(so.at[slot], out_ref.at[first + i], osem.at[slot])

    def scores(slot, t, sc, top):
        q = qv[slot, pl.ds(t * TT, TT)].reshape(ROWS, HD)
        m = None
        for j in range(3):
            s = lax.dot_general(q, kv[slot, t, j, 0], (((1,), (1,)), ((), ())), preferred_element_type=jnp.float32)
            sc[j] = s
            mj = jnp.maximum(jnp.maximum(s[:, :128], s[:, 128:256]), s[:, 256:])
            m = mj if m is None else jnp.maximum(m, mj)
            yield
        m = jnp.broadcast_to(jnp.max(m, axis=1, keepdims=True), (ROWS, HD))
        if not starts:
            m = jnp.maximum(m, si[slot, t, :, 2 * HD:])
        top[...] = m
        yield

    def weigh(i, slot, t, sc, top):
        to = lax.rem(i, 2)
        m1 = top[...]
        m = jnp.concatenate([m1] * 3, axis=1)
        acc = None
        if not starts:
            fade = jnp.exp2((si[slot, t, :, 2 * HD:] - m1) * SCALE)
            acc = si[slot, t, :, :2 * HD] * jnp.concatenate([fade, fade], axis=1)
        for j in range(3):
            p = jnp.exp2((sc[j] - m) * SCALE).astype(jnp.bfloat16)
            v2 = jnp.concatenate([kv[slot, t, j, 1], jnp.ones((ROWS, HD), jnp.bfloat16)], axis=1)
            if j == 2 * t:
                v2 = jnp.where((cut != 0) & (core == t), jnp.zeros_like(v2), v2)
            part = jnp.dot(p, v2, preferred_element_type=jnp.float32)
            acc = part if acc is None else acc + part
            yield
        if finishes:
            o = acc[:, :HD] / acc[:, HD:] * ops["gate"][t, first + i]
            ov[to, pl.ds(t * TT, TT)] = o.astype(jnp.bfloat16).reshape(TT, 8, 8, HD)
        else:
            so[to, t, :, :2 * HD] = acc
            so[to, t, :, 2 * HD:] = m1
        yield

    def both(*steps):
        for _ in itertools.zip_longest(*steps):
            pass

    def head(i, last):
        slot, ahead = lax.rem(i, 3), lax.rem(i + 1, 3)
        if not last:
            @pl.when(i + 2 < count)
            def _():
                fill(i + 2, lax.rem(i + 2, 3))

        @pl.when(i >= 2)
        def _():
            result(i - 2).wait()
        both(weigh(i, slot, 0, sc0, top0), scores(slot, 1, sc1, top1))
        if last:
            both(weigh(i, slot, 1, sc1, top1))
        else:
            filled(i + 1, ahead)
            both(weigh(i, slot, 1, sc1, top1), scores(ahead, 0, sc0, top0))
        result(i).start()

    fill(0, 0)
    if count > 1:
        fill(1, 1)
    filled(0, 0)
    both(scores(0, 0, sc0, top0))

    def step(i, _):
        head(i, False)
        return 0
    lax.fori_loop(0, count - 1, step, 0)
    head(jnp.int32(count - 1), True)
    for i in range(max(0, count - 2), count):
        result(i).wait()


def attend(name, phase, first, count, *, s, place, q, columns, halos, halo_first=0, state=None, gate=None, prev=None):
    arrays = {f"column{i}": x for i, (x, _) in enumerate(columns)}
    sides = tuple((f"column{i}", low) for i, (_, low) in enumerate(columns))
    arrays["far"], arrays["near"] = halos
    if state is not None:
        arrays["state"] = state
    if gate is not None:
        arrays["gate"] = gate
    if prev is not None:
        arrays["prev"] = prev
    names = tuple(arrays)
    heads = q.shape[3] // HD
    plan = (names, phase == 0, phase == 2, sides, PICKS[phase], halo_first)
    final = phase == 2
    shape = jax.ShapeDtypeStruct(q.shape, q.dtype) if final else jax.ShapeDtypeStruct((heads, 2, ROWS, 3 * HD), jnp.float32)
    aliases = {3 + names.index("prev"): 0} if prev is not None else {}
    return pl.pallas_call(
        functools.partial(attn_kernel, plan, first, count),
        out_shape=shape,
        in_specs=[SMEM, SMEM, ANY] + [VMEM if n == "gate" else ANY for n in names],
        out_specs=ANY,
        input_output_aliases=aliases,
        scratch_shapes=[
            pltpu.VMEM((3, 2, 3, 2, ROWS, HD), jnp.bfloat16),
            pltpu.VMEM((3, 12, 8, 8, HD), jnp.bfloat16),
            pltpu.VMEM((3, ROWS, ROWS), jnp.float32), pltpu.VMEM((3, ROWS, ROWS), jnp.float32),
            pltpu.VMEM((ROWS, HD), jnp.float32), pltpu.VMEM((ROWS, HD), jnp.float32),
            pltpu.VMEM((3, 2, ROWS, 3 * HD), jnp.float32),
            pltpu.VMEM((2, 2, ROWS, 3 * HD), jnp.float32),
            pltpu.VMEM((2, 12, 8, 8, HD), jnp.bfloat16),
            pltpu.SemaphoreType.DMA((3, 2)), pltpu.SemaphoreType.DMA((3,)),
            pltpu.SemaphoreType.DMA((3,)), pltpu.SemaphoreType.DMA((2,))],
        compiler_params=pltpu.CompilerParams(vmem_limit_bytes=60 * 2**20),
        cost_estimate=SMALL,
        name=name,
    )(s, place, q, *arrays.values())


def from_behind(block, distance):
    size = lax.axis_size("lon")
    return lax.ppermute(block, "lon", [((i - distance) % size, i) for i in range(size)])


def pairs(off):
    size = lax.axis_size("tm")
    return [[i + off, (i + off + 1) % size] for i in range(0, size, 2)]


def far_swap(x):
    route = [r for a, b in pairs(1)[:-1] for r in ((a, b), (b, a))]
    return lax.ppermute(x, "tm", route)


def near_swap(x):
    route = [r for a, b in pairs(0) for r in ((a, b), (b, a))]
    return lax.ppermute(x, "tm", route)


LAST = ((0, 3), (3, 3))


def local(query_field, key_field, value_field, tile_offsets, timesteps, gate_weight):
    heads = query_field.shape[3] // HD
    tiles = query_field.shape[0] // TT
    tm, size = lax.axis_index("tm"), lax.axis_size("tm")
    core = tm % 2
    cut = ((tm == 0) | (tm == size - 1)).astype(jnp.int32)
    shifts = tile_offsets[:, 0]
    mine = jnp.where(core == 0, shifts, shifts[::-1])
    place = jnp.stack([core, cut, far_swap(mine[:1])[0], near_swap(mine[1:])[0]])

    x = split(key_field, value_field)
    r1, l1 = from_behind(x, 1), from_behind(x, -1)

    half_freq = FREQ // 2
    frequencies = jnp.exp(-math.log(10000.0) * jnp.arange(half_freq, dtype=jnp.float32) / half_freq)
    angles = timesteps.astype(jnp.float32)[:, None] * frequencies[None, :]
    embedding = jnp.concatenate([jnp.cos(angles), jnp.sin(angles)], axis=1)
    gate_rows = jnp.dot(
        embedding, gate_weight, precision=lax.Precision.HIGHEST, preferred_element_type=jnp.float32
    ).reshape(tiles, heads, HD)

    attn = functools.partial(attend, s=tile_offsets, place=place, q=query_field)
    whole = ((0, heads),)

    (far,), (near,) = pack("edges0", 0, place, [x], whole)
    state = attn("own", 0, 0, heads, columns=[(x, 0)], halos=(far_swap(far), near_swap(near)))

    ra, la, state = lax.optimization_barrier((r1, l1, state))
    r2, l2 = from_behind(ra, 1), from_behind(la, -1)

    (far,), (near,) = pack("edges1", 1, place, [ra, la], whole)
    state = attn("next", 1, 0, heads, columns=[(r1, 0), (l1, 0)], halos=(far_swap(far), near_swap(near)), state=state)

    r2, l2, state = lax.optimization_barrier((r2, l2, state))
    fars, nears = pack("edges2", 2, place, [r2, l2, l1], LAST)
    out = None
    for (a, n), far, near in zip(LAST, fars, nears):
        out = attn(f"last_{a}", 2, a, n, columns=[(r2, 0), (l2, 0), (l1, 0)], halos=(far_swap(far), near_swap(near)),
                   halo_first=a, state=state, gate=gate_rows, prev=out)
    return out


def solution(mesh):
    return jax.shard_map(
        local,
        mesh=mesh,
        in_specs=(
            P("tm", None, "lon", "head"),
            P("tm", None, "lon", "head"),
            P("tm", None, "lon", "head"),
            P("tm", "lon"),
            P("tm"),
            P(None, "head"),
        ),
        out_specs=P("tm", None, "lon", "head"),
        check_vma=False,
    )
```

```python
import functools
import itertools
import math

import jax
import jax.numpy as jnp
from jax import lax
from jax.experimental import pallas as pl
from jax.experimental.pallas import tpu as pltpu
from jax.sharding import PartitionSpec as P

HD = 128
FREQ = 256
ROWS = 384
TT = 6
SCALE = math.log2(math.e) / math.sqrt(HD)
ANY = pl.BlockSpec(memory_space=pltpu.HBM)
SMALL = pl.CostEstimate(flops=0, bytes_accessed=1024, transcendentals=0)
VMEM = pl.BlockSpec(memory_space=pltpu.VMEM)
SMEM = pl.BlockSpec(memory_space=pltpu.SMEM)


PICKS = (lambda s: 0 * s, lambda s: jnp.where(s > 0, 1, 0), lambda s: jnp.where(s == 0, 2, jnp.where(s > 0, 1, 0)))


def split_kernel(place_ref, k_ref, v_ref, far, near, hold, into, out_of):
    core = place_ref[0]
    count = far.shape[0]
    copies, last = [], []
    for w, out in enumerate((far, near)):
        first = (core if w == 0 else 1 - core) * TT
        for i in range(count):
            for which, ref in enumerate((k_ref, v_ref)):
                source = ref.at[pl.ds(first, TT), :, :, pl.ds(i * HD, HD)]
                copies.append(pltpu.make_async_copy(source, hold.at[w, i, which], into.at[w, i, which]))
            last.append(pltpu.make_async_copy(hold.at[w, i], out.at[i], out_of.at[w, i]))
    for copy in copies:
        copy.start()
    for n, copy in enumerate(last):
        copies[2 * n].wait()
        copies[2 * n + 1].wait()
        copy.start()
    for copy in last:
        copy.wait()


def split(place, k, v):
    n = k.shape[3] // HD
    shape = jax.ShapeDtypeStruct((n, 2, TT, 8, 8, HD), k.dtype)
    parts = pl.pallas_call(
        split_kernel,
        out_shape=[shape, shape],
        in_specs=[SMEM, ANY, ANY],
        out_specs=[ANY, ANY],
        scratch_shapes=[pltpu.VMEM((2,) + shape.shape, k.dtype), pltpu.SemaphoreType.DMA((2, n, 2)), pltpu.SemaphoreType.DMA((2, n))],
        cost_estimate=SMALL,
        compiler_params=pltpu.CompilerParams(vmem_limit_bytes=60 * 2**20),
        name="split",
    )(place, k, v)
    return [x.reshape(x.shape[:2] + (ROWS, HD)) for x in parts]


def choose_kernel(pick, slot, place_ref, *refs):
    ins, (out, hold, into, out_of) = refs[:-4], refs[-4:]
    side = pick(place_ref[slot])
    count = out.shape[0]
    for c, ref in enumerate(ins):
        @pl.when(side == c)
        def _():
            for i in range(count):
                pltpu.make_async_copy(ref.at[i], hold.at[i], into.at[i]).start()
    last = [pltpu.make_async_copy(hold.at[i], out.at[i], out_of.at[i]) for i in range(count)]
    for i, copy in enumerate(last):
        pltpu.make_async_copy(hold.at[i], hold.at[i], into.at[i]).wait()
        copy.start()
    for copy in last:
        copy.wait()


def choose(name, phase, slot, place, xs):
    x = xs[0]
    return pl.pallas_call(
        functools.partial(choose_kernel, PICKS[phase], slot),
        out_shape=jax.ShapeDtypeStruct(x.shape, x.dtype),
        in_specs=[SMEM] + [ANY] * len(xs),
        out_specs=ANY,
        scratch_shapes=[pltpu.VMEM(x.shape, x.dtype), pltpu.SemaphoreType.DMA(x.shape[:1]), pltpu.SemaphoreType.DMA(x.shape[:1])],
        cost_estimate=SMALL,
        compiler_params=pltpu.CompilerParams(vmem_limit_bytes=60 * 2**20),
        name=name,
    )(place, *xs)


def attn_kernel(plan, first, count, s_ref, place_ref, q_ref, *refs):
    names, starts, finishes, sides, pick = plan
    ops = dict(zip(names, refs))
    out_ref, kv, qv, sc0, sc1, top0, top1, si, so, ov, ksem, qsem, isem, osem = refs[len(refs) - 14:]
    core, cut = place_ref[0], place_ref[1]

    def fill(i, slot):
        h = first + i
        for t in range(2):
            side = pick(s_ref[t, 0])
            halo = kv.at[slot, t, 2 * t]
            for c in range(sides):
                far, near = ops[f"far{c}"].at[h], ops[f"near{c}"].at[h]

                @pl.when(side == c)
                def _():
                    pltpu.make_async_copy(far, kv.at[slot, t, 1 - t + core], ksem.at[slot, t]).start()
                    pltpu.make_async_copy(near, kv.at[slot, t, 2 - t - core], ksem.at[slot, t]).start()

                @pl.when((side == c) & (core == t) & (cut != 0))
                def _():
                    pltpu.make_async_copy(far, halo, ksem.at[slot, t]).start()

            @pl.when((core == t) & (cut == 0))
            def _():
                pltpu.make_async_copy(ops["far"].at[h], halo, ksem.at[slot, t]).start()

            @pl.when(core != t)
            def _():
                pltpu.make_async_copy(ops["near"].at[h], halo, ksem.at[slot, t]).start()
        q_copy(i, slot).start()
        if not starts:
            state_in(i, slot).start()

    def filled(i, slot):
        for t in range(2):
            pltpu.make_async_copy(kv.at[slot, t], kv.at[slot, t], ksem.at[slot, t]).wait()
        q_copy(i, slot).wait()
        if not starts:
            state_in(i, slot).wait()

    def lanes(i):
        return pl.ds(pl.multiple_of((first + i) * HD, HD), HD)

    def q_copy(i, slot):
        return pltpu.make_async_copy(q_ref.at[:, :, :, lanes(i)], qv.at[slot], qsem.at[slot])

    def state_in(i, slot):
        return pltpu.make_async_copy(ops["state"].at[first + i], si.at[slot], isem.at[slot])

    def result(i):
        slot = lax.rem(i, 2)
        if finishes:
            return pltpu.make_async_copy(ov.at[slot], out_ref.at[:, :, :, lanes(i)], osem.at[slot])
        return pltpu.make_async_copy(so.at[slot], out_ref.at[first + i], osem.at[slot])

    def scores(slot, t, sc, top):
        q = qv[slot, pl.ds(t * TT, TT)].reshape(ROWS, HD)
        m = None
        for j in range(3):
            s = lax.dot_general(q, kv[slot, t, j, 0], (((1,), (1,)), ((), ())), preferred_element_type=jnp.float32)
            sc[j] = s
            mj = jnp.maximum(jnp.maximum(s[:, :128], s[:, 128:256]), s[:, 256:])
            m = mj if m is None else jnp.maximum(m, mj)
            yield
        m = jnp.broadcast_to(jnp.max(m, axis=1, keepdims=True), (ROWS, HD))
        if not starts:
            m = jnp.maximum(m, si[slot, t, :, 2 * HD:])
        top[...] = m
        yield

    def weigh(i, slot, t, sc, top):
        to = lax.rem(i, 2)
        m1 = top[...]
        m = jnp.concatenate([m1] * 3, axis=1)
        acc = None
        if not starts:
            fade = jnp.exp2((si[slot, t, :, 2 * HD:] - m1) * SCALE)
            acc = si[slot, t, :, :2 * HD] * jnp.concatenate([fade, fade], axis=1)
        for j in range(3):
            p = jnp.exp2((sc[j] - m) * SCALE).astype(jnp.bfloat16)
            v2 = jnp.concatenate([kv[slot, t, j, 1], jnp.ones((ROWS, HD), jnp.bfloat16)], axis=1)
            if j == 2 * t:
                v2 = jnp.where((cut != 0) & (core == t), jnp.zeros_like(v2), v2)
            part = jnp.dot(p, v2, preferred_element_type=jnp.float32)
            acc = part if acc is None else acc + part
            yield
        if finishes:
            o = acc[:, :HD] / acc[:, HD:] * ops["gate"][t, first + i]
            ov[to, pl.ds(t * TT, TT)] = o.astype(jnp.bfloat16).reshape(TT, 8, 8, HD)
        else:
            so[to, t, :, :2 * HD] = acc
            so[to, t, :, 2 * HD:] = m1
        yield

    def both(*steps):
        for _ in itertools.zip_longest(*steps):
            pass

    def head(i, last):
        slot, ahead = lax.rem(i, 3), lax.rem(i + 1, 3)
        if not last:
            @pl.when(i + 2 < count)
            def _():
                fill(i + 2, lax.rem(i + 2, 3))

        @pl.when(i >= 2)
        def _():
            result(i - 2).wait()
        both(weigh(i, slot, 0, sc0, top0), scores(slot, 1, sc1, top1))
        if last:
            both(weigh(i, slot, 1, sc1, top1))
        else:
            filled(i + 1, ahead)
            both(weigh(i, slot, 1, sc1, top1), scores(ahead, 0, sc0, top0))
        result(i).start()

    fill(0, 0)
    if count > 1:
        fill(1, 1)
    filled(0, 0)
    both(scores(0, 0, sc0, top0))

    def step(i, _):
        head(i, False)
        return 0
    lax.fori_loop(0, count - 1, step, 0)
    head(jnp.int32(count - 1), True)
    for i in range(max(0, count - 2), count):
        result(i).wait()


def attend(name, phase, first, count, *, s, place, q, columns, halos, state=None, gate=None, prev=None):
    arrays, sides = {}, len(columns)
    for c, (far, near) in enumerate(columns):
        arrays[f"far{c}"], arrays[f"near{c}"] = far, near
    arrays["far"], arrays["near"] = halos
    if state is not None:
        arrays["state"] = state
    if gate is not None:
        arrays["gate"] = gate
    if prev is not None:
        arrays["prev"] = prev
    names = tuple(arrays)
    heads = q.shape[3] // HD
    plan = (names, phase == 0, phase == 2, sides, PICKS[phase])
    final = phase == 2
    shape = jax.ShapeDtypeStruct(q.shape, q.dtype) if final else jax.ShapeDtypeStruct((heads, 2, ROWS, 3 * HD), jnp.float32)
    aliases = {3 + names.index("prev"): 0} if prev is not None else {}
    return pl.pallas_call(
        functools.partial(attn_kernel, plan, first, count),
        out_shape=shape,
        in_specs=[SMEM, SMEM, ANY] + [VMEM if n == "gate" else ANY for n in names],
        out_specs=ANY,
        input_output_aliases=aliases,
        scratch_shapes=[
            pltpu.VMEM((3, 2, 3, 2, ROWS, HD), jnp.bfloat16),
            pltpu.VMEM((3, 12, 8, 8, HD), jnp.bfloat16),
            pltpu.VMEM((3, ROWS, ROWS), jnp.float32), pltpu.VMEM((3, ROWS, ROWS), jnp.float32),
            pltpu.VMEM((ROWS, HD), jnp.float32), pltpu.VMEM((ROWS, HD), jnp.float32),
            pltpu.VMEM((3, 2, ROWS, 3 * HD), jnp.float32),
            pltpu.VMEM((2, 2, ROWS, 3 * HD), jnp.float32),
            pltpu.VMEM((2, 12, 8, 8, HD), jnp.bfloat16),
            pltpu.SemaphoreType.DMA((3, 2)), pltpu.SemaphoreType.DMA((3,)),
            pltpu.SemaphoreType.DMA((3,)), pltpu.SemaphoreType.DMA((2,))],
        compiler_params=pltpu.CompilerParams(vmem_limit_bytes=60 * 2**20),
        cost_estimate=SMALL,
        name=name,
    )(s, place, q, *arrays.values())


def from_behind(block, distance):
    size = lax.axis_size("lon")
    return lax.ppermute(block, "lon", [((i - distance) % size, i) for i in range(size)])


def pairs(off):
    size = lax.axis_size("tm")
    return [[i + off, (i + off + 1) % size] for i in range(0, size, 2)]


def far_swap(x):
    route = [r for a, b in pairs(1)[:-1] for r in ((a, b), (b, a))]
    return lax.ppermute(x, "tm", route)


def near_swap(x):
    route = [r for a, b in pairs(0) for r in ((a, b), (b, a))]
    return lax.ppermute(x, "tm", route)


def local(query_field, key_field, value_field, tile_offsets, timesteps, gate_weight):
    heads = query_field.shape[3] // HD
    tiles = query_field.shape[0] // TT
    tm, size = lax.axis_index("tm"), lax.axis_size("tm")
    core = tm % 2
    cut = ((tm == 0) | (tm == size - 1)).astype(jnp.int32)
    shifts = tile_offsets[:, 0]
    mine = jnp.where(core == 0, shifts, shifts[::-1])
    place = jnp.stack([core, cut, far_swap(mine[:1])[0], near_swap(mine[1:])[0]])

    xf, xn = split(jnp.stack([core]), key_field, value_field)
    rf, lf = from_behind(xf, 1), from_behind(xf, -1)
    rn, ln = from_behind(xn, 1), from_behind(xn, -1)
    r2f, l2f = from_behind(rf, 1), from_behind(lf, -1)
    r2n, l2n = from_behind(rn, 1), from_behind(ln, -1)

    half_freq = FREQ // 2
    frequencies = jnp.exp(-math.log(10000.0) * jnp.arange(half_freq, dtype=jnp.float32) / half_freq)
    angles = timesteps.astype(jnp.float32)[:, None] * frequencies[None, :]
    embedding = jnp.concatenate([jnp.cos(angles), jnp.sin(angles)], axis=1)
    gate_rows = jnp.dot(
        embedding, gate_weight, precision=lax.Precision.HIGHEST, preferred_element_type=jnp.float32
    ).reshape(tiles, heads, HD)

    attn = functools.partial(attend, s=tile_offsets, place=place, q=query_field)
    state = attn("own", 0, 0, heads, columns=[(xf, xn)], halos=(far_swap(xf), near_swap(xn)))

    rf_, lf_, rn_, ln_, state = lax.optimization_barrier((rf, lf, rn, ln, state))
    far = far_swap(choose("far1", 1, 2, place, [rf_, lf_]))
    near = near_swap(choose("near1", 1, 3, place, [rn_, ln_]))
    far2 = choose("far2", 2, 2, place, [r2f, l2f, lf])
    state, far2, gate_rows = lax.optimization_barrier((state, far2, gate_rows))
    state = attn("next", 1, 0, heads, columns=[(rf, rn), (lf, ln)], halos=(far, near), state=state)

    r2n_, l2n_, state = lax.optimization_barrier((r2n, l2n, state))
    near2, far2 = lax.optimization_barrier((choose("near2", 2, 3, place, [r2n_, l2n_, ln]), far_swap(far2)))
    return attn("last", 2, 0, heads, columns=[(r2f, r2n), (l2f, l2n), (lf, ln)], halos=(far2, near_swap(near2)),
                state=state, gate=gate_rows)


def solution(mesh):
    return jax.shard_map(
        local,
        mesh=mesh,
        in_specs=(
            P("tm", None, "lon", "head"),
            P("tm", None, "lon", "head"),
            P("tm", None, "lon", "head"),
            P("tm", "lon"),
            P("tm"),
            P(None, "head"),
        ),
        out_specs=P("tm", None, "lon", "head"),
        check_vma=False,
    )
```

```python
import functools
import itertools
import math

import jax
import jax.numpy as jnp
from jax import lax
from jax.experimental import pallas as pl
from jax.experimental.pallas import tpu as pltpu
from jax.sharding import PartitionSpec as P

HD = 128
FREQ = 256
ROWS = 384
TT = 6
SCALE = math.log2(math.e) / math.sqrt(HD)
ANY = pl.BlockSpec(memory_space=pltpu.HBM)
SMALL = pl.CostEstimate(flops=0, bytes_accessed=1024, transcendentals=0)
VMEM = pl.BlockSpec(memory_space=pltpu.VMEM)
SMEM = pl.BlockSpec(memory_space=pltpu.SMEM)


PICKS = (lambda s: 0 * s, lambda s: jnp.where(s > 0, 1, 0), lambda s: jnp.where(s == 0, 2, jnp.where(s > 0, 1, 0)))


def split_kernel(far, place_ref, k_ref, v_ref, out, hold, into, out_of):
    core = place_ref[0]
    first = (core if far else 1 - core) * TT
    count = out.shape[0]
    last = []
    for i in range(count):
        for which, ref in enumerate((k_ref, v_ref)):
            source = ref.at[pl.ds(first, TT), :, :, pl.ds(i * HD, HD)]
            pltpu.make_async_copy(source, hold.at[i, which], into.at[i]).start()
        last.append(pltpu.make_async_copy(hold.at[i], out.at[i], out_of.at[i]))
    for i, copy in enumerate(last):
        pltpu.make_async_copy(hold.at[i], hold.at[i], into.at[i]).wait()
        copy.start()
    for copy in last:
        copy.wait()


def split(name, far, place, k, v):
    n = k.shape[3] // HD
    x = pl.pallas_call(
        functools.partial(split_kernel, far),
        out_shape=jax.ShapeDtypeStruct((n, 2, TT, 8, 8, HD), k.dtype),
        in_specs=[SMEM, ANY, ANY],
        out_specs=ANY,
        scratch_shapes=[pltpu.VMEM((n, 2, TT, 8, 8, HD), k.dtype), pltpu.SemaphoreType.DMA((n,)), pltpu.SemaphoreType.DMA((n,))],
        cost_estimate=SMALL,
        compiler_params=pltpu.CompilerParams(vmem_limit_bytes=60 * 2**20),
        name=name,
    )(place, k, v)
    return x.reshape(n, 2, ROWS, HD)


def hand_on_kernel(x_ref, *refs):
    out = refs[-1]
    for i in range(out.shape[0]):
        out[i] = x_ref[i]


def hand_on(x, *others):
    return pl.pallas_call(
        hand_on_kernel,
        out_shape=jax.ShapeDtypeStruct(x.shape, x.dtype),
        in_specs=[SMEM] + [ANY] * len(others),
        out_specs=SMEM,
        cost_estimate=SMALL,
        compiler_params=pltpu.CompilerParams(vmem_limit_bytes=60 * 2**20),
        name="hand_on",
    )(x, *others)


def choose_kernel(pick, slot, place_ref, *refs):
    ins, (out, hold, into, out_of) = refs[:-4], refs[-4:]
    side = pick(place_ref[slot])
    count = out.shape[0]
    for c, ref in enumerate(ins):
        @pl.when(side == c)
        def _():
            for i in range(count):
                pltpu.make_async_copy(ref.at[i], hold.at[i], into.at[i]).start()
    last = [pltpu.make_async_copy(hold.at[i], out.at[i], out_of.at[i]) for i in range(count)]
    for i, copy in enumerate(last):
        pltpu.make_async_copy(hold.at[i], hold.at[i], into.at[i]).wait()
        copy.start()
    for copy in last:
        copy.wait()


def choose(name, phase, slot, place, xs):
    x = xs[0]
    return pl.pallas_call(
        functools.partial(choose_kernel, PICKS[phase], slot),
        out_shape=jax.ShapeDtypeStruct(x.shape, x.dtype),
        in_specs=[SMEM] + [ANY] * len(xs),
        out_specs=ANY,
        scratch_shapes=[pltpu.VMEM(x.shape, x.dtype), pltpu.SemaphoreType.DMA(x.shape[:1]), pltpu.SemaphoreType.DMA(x.shape[:1])],
        cost_estimate=SMALL,
        compiler_params=pltpu.CompilerParams(vmem_limit_bytes=60 * 2**20),
        name=name,
    )(place, *xs)


def attn_kernel(plan, first, count, s_ref, place_ref, q_ref, *refs):
    names, starts, finishes, phases = plan
    blocks = [[(phase, b) for phase in phases for b in letters] for letters in ("EFN", "FNM")]
    ops = dict(zip(names, refs))
    out_ref, kv, qv, sc, top, si, so, ov, ksem, qsem, isem, osem = refs[len(refs) - 12:]
    core, cut = place_ref[0], place_ref[1]
    tiles = (core, 1 - core)
    width = [len(b) * ROWS for b in blocks]
    base = (0, len(blocks[0]))

    def fill(i, slot):
        h = first + i
        for u in range(2):
            for j, ((phase, sides), block) in enumerate(blocks[u]):
                side = PICKS[phase](s_ref[tiles[u], 0])
                to = kv.at[slot, :, base[u] + j]
                sem = ksem.at[slot, u]
                if block == "M":
                    pltpu.make_async_copy(ops[f"M{phase}"].at[h], to, sem).start()
                    continue
                if block == "E":
                    @pl.when(cut == 0)
                    def _():
                        pltpu.make_async_copy(ops[f"E{phase}"].at[h], to, sem).start()
                for c in range(sides):
                    name = f"{'N' if block == 'N' else 'F'}{phase}{c}"

                    @pl.when((side == c) & ((cut != 0) if block == "E" else True))
                    def _():
                        pltpu.make_async_copy(ops[name].at[h], to, sem).start()
        q_copy(i, slot).start()
        if not starts:
            state_in(i, slot).start()

    def filled(i, slot):
        for u in range(2):
            whole = kv.at[slot, :, pl.ds(base[u], len(blocks[u]))]
            pltpu.make_async_copy(whole, whole, ksem.at[slot, u]).wait()
        q_copy(i, slot).wait()
        if not starts:
            state_in(i, slot).wait()

    def lanes(i):
        return pl.ds(pl.multiple_of((first + i) * HD, HD), HD)

    def q_copy(i, slot):
        return pltpu.make_async_copy(q_ref.at[:, :, :, lanes(i)], qv.at[slot], qsem.at[slot])

    def state_in(i, slot):
        return pltpu.make_async_copy(ops["state"].at[first + i], si.at[slot], isem.at[slot])

    def result(i):
        slot = lax.rem(i, 2)
        if finishes:
            return pltpu.make_async_copy(ov.at[slot], out_ref.at[:, :, :, lanes(i)], osem.at[slot])
        return pltpu.make_async_copy(so.at[slot], out_ref.at[first + i], osem.at[slot])

    def stacked(slot, which, u):
        return kv[slot, which, base[u]:base[u] + len(blocks[u])].reshape(width[u], HD)

    def scores(slot, u, sc, top):
        k = stacked(slot, 0, u)
        step = ROWS
        for r in range(0, ROWS, step):
            q = qv[slot, pl.ds(tiles[u] * TT + r // 64, step // 64)].reshape(step, HD)
            s = lax.dot_general(q, k, (((1,), (1,)), ((), ())), preferred_element_type=jnp.float32)
            sc[r:r + step, :width[u]] = s
            m = s[:, :HD]
            for c in range(HD, width[u], HD):
                m = jnp.maximum(m, s[:, c:c + HD])
            m = jnp.broadcast_to(jnp.max(m, axis=1, keepdims=True), (step, HD))
            if not starts:
                m = jnp.maximum(m, jnp.broadcast_to(si[slot, u, r:r + step, HD:HD + 1], (step, HD)))
            top[r:r + step] = m
            yield

    def weigh(i, slot, u, sc, top):
        to = lax.rem(i, 2)
        v2 = []
        for j, (_, block) in enumerate(blocks[u]):
            v = jnp.concatenate([kv[slot, 1, base[u] + j], jnp.ones((ROWS, HD), jnp.bfloat16)], axis=1)
            v2.append(jnp.where(cut != 0, jnp.zeros_like(v), v) if block == "E" else v)
        v2 = jnp.concatenate(v2, axis=0)
        step = ROWS
        for r in range(0, ROWS, step):
            m1 = top[r:r + step]
            m = jnp.concatenate([m1] * (width[u] // HD), axis=1)
            p = jnp.exp2((sc[r:r + step, :width[u]] - m) * SCALE).astype(jnp.bfloat16)
            acc = jnp.dot(p, v2, preferred_element_type=jnp.float32)
            if not starts:
                old = si[slot, u, r:r + step, HD:]
                fade = jnp.exp2((jnp.broadcast_to(old[:, :1], (step, HD)) - m1) * SCALE)
                total = jnp.broadcast_to(old[:, HD - 1:], (step, HD))
                acc += jnp.concatenate([si[slot, u, r:r + step, :HD], total], axis=1) * jnp.concatenate([fade, fade], axis=1)
            if finishes:
                o = acc[:, :HD] / acc[:, HD:] * ops["gate"][tiles[u], first + i]
                ov[to, pl.ds(tiles[u] * TT + r // 64, step // 64)] = o.astype(jnp.bfloat16).reshape(step // 64, 8, 8, HD)
            else:
                lane = lax.broadcasted_iota(jnp.int32, (step, HD), 1)
                so[to, u, r:r + step, :HD] = acc[:, :HD]
                so[to, u, r:r + step, HD:] = jnp.where(lane < HD // 2, m1, acc[:, HD:])
            yield

    def both(*steps):
        for _ in itertools.zip_longest(*steps):
            pass

    def head(i, par, last):
        slot, ahead = lax.rem(i, 3), lax.rem(i + 1, 3)
        if not last:
            @pl.when(i + 2 < count)
            def _():
                fill(i + 2, lax.rem(i + 2, 3))

        @pl.when(i >= 2)
        def _():
            result(i - 2).wait()
        steps = [weigh(i, slot, u, sc.at[par, u], top.at[par, u]) for u in range(2)]
        if not last:
            filled(i + 1, ahead)
            steps += [scores(ahead, u, sc.at[1 - par, u], top.at[1 - par, u]) for u in range(2)]
        both(*steps)
        result(i).start()

    fill(0, 0)
    if count > 1:
        fill(1, 1)
    filled(0, 0)
    both(*[scores(0, u, sc.at[0, u], top.at[0, u]) for u in range(2)])

    def pair(p, _):
        head(2 * p, 0, False)
        head(2 * p + 1, 1, False)
        return 0
    lax.fori_loop(0, (count - 1) // 2, pair, 0)
    if count % 2 == 0:
        head(jnp.int32(count - 2), 0, False)
    head(jnp.int32(count - 1), (count - 1) % 2, True)
    for i in range(max(0, count - 2), count):
        result(i).wait()


def attend(name, parts, *, s, place, q, state=None, gate=None):
    arrays, phases = {}, []
    for phase, columns, halos in parts:
        phases.append((phase, len(columns)))
        for c, (far, near) in enumerate(columns):
            arrays[f"F{phase}{c}"], arrays[f"N{phase}{c}"] = far, near
        arrays[f"E{phase}"], arrays[f"M{phase}"] = halos
    arrays.update(state=state, gate=gate)
    arrays = {n: x for n, x in arrays.items() if x is not None}
    names = tuple(arrays)
    heads = q.shape[3] // HD
    plan = (names, state is None, gate is not None, phases)
    shape = jax.ShapeDtypeStruct((heads, 2, ROWS, 2 * HD), jnp.float32)
    if gate is not None:
        shape = jax.ShapeDtypeStruct(q.shape, q.dtype)
    blocks = 3 * len(phases)
    return pl.pallas_call(
        functools.partial(attn_kernel, plan, 0, heads),
        out_shape=shape,
        in_specs=[SMEM, SMEM, ANY] + [VMEM if n == "gate" else ANY for n in names],
        out_specs=ANY,
        scratch_shapes=[
            pltpu.VMEM((3, 2, 2 * blocks, ROWS, HD), jnp.bfloat16),
            pltpu.VMEM((3, 12, 8, 8, HD), jnp.bfloat16),
            pltpu.VMEM((2, 2, ROWS, blocks * ROWS), jnp.float32),
            pltpu.VMEM((2, 2, ROWS, HD), jnp.float32),
            pltpu.VMEM((3, 2, ROWS, 2 * HD), jnp.float32),
            pltpu.VMEM((2, 2, ROWS, 2 * HD), jnp.float32),
            pltpu.VMEM((2, 12, 8, 8, HD), jnp.bfloat16),
            pltpu.SemaphoreType.DMA((3, 2)), pltpu.SemaphoreType.DMA((3,)),
            pltpu.SemaphoreType.DMA((3,)), pltpu.SemaphoreType.DMA((2,))],
        compiler_params=pltpu.CompilerParams(vmem_limit_bytes=60 * 2**20),
        cost_estimate=SMALL,
        name=name,
    )(s, place, q, *arrays.values())


def from_behind(block, distance):
    size = lax.axis_size("lon")
    return lax.ppermute(block, "lon", [((i - distance) % size, i) for i in range(size)])


def pairs(off):
    size = lax.axis_size("tm")
    return [[i + off, (i + off + 1) % size] for i in range(0, size, 2)]


def far_swap(x):
    route = [r for a, b in pairs(1)[:-1] for r in ((a, b), (b, a))]
    return lax.ppermute(x, "tm", route)


def near_swap(x):
    route = [r for a, b in pairs(0) for r in ((a, b), (b, a))]
    return lax.ppermute(x, "tm", route)


def local(query_field, key_field, value_field, tile_offsets, timesteps, gate_weight):
    heads = query_field.shape[3] // HD
    tiles = query_field.shape[0] // TT
    tm, size = lax.axis_index("tm"), lax.axis_size("tm")
    core = tm % 2
    cut = ((tm == 0) | (tm == size - 1)).astype(jnp.int32)
    shifts = tile_offsets[:, 0]
    mine = jnp.where(core == 0, shifts, shifts[::-1])
    place = jnp.stack([core, cut, far_swap(mine[:1])[0], near_swap(mine[1:])[0]])

    at = jnp.stack([core])
    xf = split("split_far", True, at, key_field, value_field)
    rf, lf = from_behind(xf, 1), from_behind(xf, -1)
    xn = split("split_near", False, at, key_field, value_field)
    rn, ln = from_behind(xn, 1), from_behind(xn, -1)
    r2f, l2f = from_behind(rf, 1), from_behind(lf, -1)
    r2n, l2n = from_behind(rn, 1), from_behind(ln, -1)

    half_freq = FREQ // 2
    frequencies = jnp.exp(-math.log(10000.0) * jnp.arange(half_freq, dtype=jnp.float32) / half_freq)
    angles = timesteps.astype(jnp.float32)[:, None] * frequencies[None, :]
    embedding = jnp.concatenate([jnp.cos(angles), jnp.sin(angles)], axis=1)
    gate_rows = jnp.dot(
        embedding, gate_weight, precision=lax.Precision.HIGHEST, preferred_element_type=jnp.float32
    ).reshape(tiles, heads, HD)

    attn = functools.partial(attend, s=tile_offsets, place=place, q=query_field)
    far0, near0 = far_swap(xf), near_swap(xn)
    later = hand_on(place, far0, near0)
    far1 = far_swap(choose("far1", 1, 2, later, [rf, lf]))
    near1 = near_swap(choose("near1", 1, 3, later, [rn, ln]))
    far2 = choose("far2", 2, 2, place, [r2f, l2f, lf])
    far1, far2, gate_rows = lax.optimization_barrier((far1, far2, gate_rows))
    parts = [(0, [(xf, xn)], (far0, near0)), (1, [(rf, rn), (lf, ln)], (far1, near1))]
    state = attn("first", parts)

    r2n_, l2n_, state = lax.optimization_barrier((r2n, l2n, state))
    near2, far2 = lax.optimization_barrier((choose("near2", 2, 3, place, [r2n_, l2n_, ln]), far_swap(far2)))
    parts = [(2, [(r2f, r2n), (l2f, l2n), (lf, ln)], (far2, near_swap(near2)))]
    return attn("last", parts, state=state, gate=gate_rows)


def solution(mesh):
    return jax.shard_map(
        local,
        mesh=mesh,
        in_specs=(
            P("tm", None, "lon", "head"),
            P("tm", None, "lon", "head"),
            P("tm", None, "lon", "head"),
            P("tm", "lon"),
            P("tm"),
            P(None, "head"),
        ),
        out_specs=P("tm", None, "lon", "head"),
        check_vma=False,
    )
```

```python
import functools
import itertools
import math

import jax
import jax.numpy as jnp
from jax import lax
from jax.experimental import pallas as pl
from jax.experimental.pallas import tpu as pltpu
from jax.sharding import PartitionSpec as P

HD = 128
FREQ = 256
ROWS = 384
TT = 6
SCALE = math.log2(math.e) / math.sqrt(HD)
ANY = pl.BlockSpec(memory_space=pltpu.HBM)
SMALL = pl.CostEstimate(flops=0, bytes_accessed=1024, transcendentals=0)
VMEM = pl.BlockSpec(memory_space=pltpu.VMEM)
SMEM = pl.BlockSpec(memory_space=pltpu.SMEM)


PICKS = (lambda s: 0 * s, lambda s: jnp.where(s > 0, 1, 0), lambda s: jnp.where(s == 0, 2, jnp.where(s > 0, 1, 0)))


def split_kernel(far, place_ref, k_ref, v_ref, out, hold, into, out_of):
    core = place_ref[0]
    first = (core if far else 1 - core) * TT
    count = out.shape[0]
    last = []
    for i in range(count):
        for which, ref in enumerate((k_ref, v_ref)):
            source = ref.at[pl.ds(first, TT), :, :, pl.ds(i * HD, HD)]
            pltpu.make_async_copy(source, hold.at[i, which], into.at[i]).start()
        last.append(pltpu.make_async_copy(hold.at[i], out.at[i], out_of.at[i]))
    for i, copy in enumerate(last):
        pltpu.make_async_copy(hold.at[i], hold.at[i], into.at[i]).wait()
        copy.start()
    for copy in last:
        copy.wait()


def split(name, far, place, k, v):
    n = k.shape[3] // HD
    x = pl.pallas_call(
        functools.partial(split_kernel, far),
        out_shape=jax.ShapeDtypeStruct((n, 2, TT, 8, 8, HD), k.dtype),
        in_specs=[SMEM, ANY, ANY],
        out_specs=ANY,
        scratch_shapes=[pltpu.VMEM((n, 2, TT, 8, 8, HD), k.dtype), pltpu.SemaphoreType.DMA((n,)), pltpu.SemaphoreType.DMA((n,))],
        cost_estimate=SMALL,
        compiler_params=pltpu.CompilerParams(vmem_limit_bytes=60 * 2**20),
        name=name,
    )(place, k, v)
    return x.reshape(n, 2, ROWS, HD)


def hand_on_kernel(x_ref, *refs):
    out = refs[-1]
    for i in range(out.shape[0]):
        out[i] = x_ref[i]


def hand_on(x, *others):
    return pl.pallas_call(
        hand_on_kernel,
        out_shape=jax.ShapeDtypeStruct(x.shape, x.dtype),
        in_specs=[SMEM] + [ANY] * len(others),
        out_specs=SMEM,
        cost_estimate=SMALL,
        compiler_params=pltpu.CompilerParams(vmem_limit_bytes=60 * 2**20),
        name="hand_on",
    )(x, *others)


def choose_kernel(pick, slot, place_ref, *refs):
    ins, (out, hold, into, out_of) = refs[:-4], refs[-4:]
    side = pick(place_ref[slot])
    count = out.shape[0]
    for c, ref in enumerate(ins):
        @pl.when(side == c)
        def _():
            for i in range(count):
                pltpu.make_async_copy(ref.at[i], hold.at[i], into.at[i]).start()
    last = [pltpu.make_async_copy(hold.at[i], out.at[i], out_of.at[i]) for i in range(count)]
    for i, copy in enumerate(last):
        pltpu.make_async_copy(hold.at[i], hold.at[i], into.at[i]).wait()
        copy.start()
    for copy in last:
        copy.wait()


def choose(name, phase, slot, place, xs):
    x = xs[0]
    return pl.pallas_call(
        functools.partial(choose_kernel, PICKS[phase], slot),
        out_shape=jax.ShapeDtypeStruct(x.shape, x.dtype),
        in_specs=[SMEM] + [ANY] * len(xs),
        out_specs=ANY,
        scratch_shapes=[pltpu.VMEM(x.shape, x.dtype), pltpu.SemaphoreType.DMA(x.shape[:1]), pltpu.SemaphoreType.DMA(x.shape[:1])],
        cost_estimate=SMALL,
        compiler_params=pltpu.CompilerParams(vmem_limit_bytes=60 * 2**20),
        name=name,
    )(place, *xs)


def attn_kernel(plan, first, count, s_ref, place_ref, q_ref, *refs):
    names, starts, finishes, phases = plan
    blocks = [[(phase, b) for phase in phases for b in letters] for letters in ("EFN", "FNM")]
    ops = dict(zip(names, refs))
    out_ref, kv, qv, sc, top, si, so, ov, ksem, qsem, isem, osem = refs[len(refs) - 12:]
    core, cut = place_ref[0], place_ref[1]
    tiles = (core, 1 - core)
    width = [len(b) * ROWS for b in blocks]
    base = (0, len(blocks[0]))

    def fill(i, slot):
        h = first + i
        for u in range(2):
            for j, ((phase, sides), block) in enumerate(blocks[u]):
                side = PICKS[phase](s_ref[tiles[u], 0])
                to = kv.at[slot, :, base[u] + j]
                sem = ksem.at[slot, u]
                if block == "M":
                    pltpu.make_async_copy(ops[f"M{phase}"].at[h], to, sem).start()
                    continue
                if block == "E":
                    @pl.when(cut == 0)
                    def _():
                        pltpu.make_async_copy(ops[f"E{phase}"].at[h], to, sem).start()
                for c in range(sides):
                    name = f"{'N' if block == 'N' else 'F'}{phase}{c}"

                    @pl.when((side == c) & ((cut != 0) if block == "E" else True))
                    def _():
                        pltpu.make_async_copy(ops[name].at[h], to, sem).start()
        q_copy(i, slot).start()
        if not starts:
            state_in(i, slot).start()

    def filled(i, slot):
        for u in range(2):
            whole = kv.at[slot, :, pl.ds(base[u], len(blocks[u]))]
            pltpu.make_async_copy(whole, whole, ksem.at[slot, u]).wait()
        q_copy(i, slot).wait()
        if not starts:
            state_in(i, slot).wait()

    def lanes(i):
        return pl.ds(pl.multiple_of((first + i) * HD, HD), HD)

    def q_copy(i, slot):
        return pltpu.make_async_copy(q_ref.at[:, :, :, lanes(i)], qv.at[slot], qsem.at[slot])

    def state_in(i, slot):
        return pltpu.make_async_copy(ops["state"].at[first + i], si.at[slot], isem.at[slot])

    def result(i):
        slot = lax.rem(i, 2)
        if finishes:
            return pltpu.make_async_copy(ov.at[slot], out_ref.at[:, :, :, lanes(i)], osem.at[slot])
        return pltpu.make_async_copy(so.at[slot], out_ref.at[first + i], osem.at[slot])

    def stacked(slot, which, u):
        return kv[slot, which, base[u]:base[u] + len(blocks[u])].reshape(width[u], HD)

    def scores(slot, u, sc, top):
        k = stacked(slot, 0, u)
        step = ROWS
        for r in range(0, ROWS, step):
            q = qv[slot, pl.ds(tiles[u] * TT + r // 64, step // 64)].reshape(step, HD)
            s = lax.dot_general(q, k, (((1,), (1,)), ((), ())), preferred_element_type=jnp.float32)
            sc[r:r + step, :width[u]] = s
            m = s[:, :HD]
            for c in range(HD, width[u], HD):
                m = jnp.maximum(m, s[:, c:c + HD])
            m = jnp.broadcast_to(jnp.max(m, axis=1, keepdims=True), (step, HD))
            if not starts:
                m = jnp.maximum(m, jnp.broadcast_to(si[slot, u, r:r + step, HD:HD + 1], (step, HD)))
            top[r:r + step] = m
            yield

    def weigh(i, slot, u, sc, top):
        to = lax.rem(i, 2)
        v2 = []
        for j, (_, block) in enumerate(blocks[u]):
            v = jnp.concatenate([kv[slot, 1, base[u] + j], jnp.ones((ROWS, HD), jnp.bfloat16)], axis=1)
            v2.append(jnp.where(cut != 0, jnp.zeros_like(v), v) if block == "E" else v)
        v2 = jnp.concatenate(v2, axis=0)
        step = ROWS
        for r in range(0, ROWS, step):
            m1 = top[r:r + step]
            m = jnp.concatenate([m1] * (width[u] // HD), axis=1)
            p = jnp.exp2((sc[r:r + step, :width[u]] - m) * SCALE).astype(jnp.bfloat16)
            acc = jnp.dot(p, v2, preferred_element_type=jnp.float32)
            if not starts:
                old = si[slot, u, r:r + step, HD:]
                fade = jnp.exp2((jnp.broadcast_to(old[:, :1], (step, HD)) - m1) * SCALE)
                total = jnp.broadcast_to(old[:, HD - 1:], (step, HD))
                acc += jnp.concatenate([si[slot, u, r:r + step, :HD], total], axis=1) * jnp.concatenate([fade, fade], axis=1)
            if finishes:
                o = acc[:, :HD] / acc[:, HD:] * ops["gate"][tiles[u], first + i]
                ov[to, pl.ds(tiles[u] * TT + r // 64, step // 64)] = o.astype(jnp.bfloat16).reshape(step // 64, 8, 8, HD)
            else:
                lane = lax.broadcasted_iota(jnp.int32, (step, HD), 1)
                so[to, u, r:r + step, :HD] = acc[:, :HD]
                so[to, u, r:r + step, HD:] = jnp.where(lane < HD // 2, m1, acc[:, HD:])
            yield

    def both(*steps):
        for _ in itertools.zip_longest(*steps):
            pass

    def head(i, par, last):
        slot, ahead = lax.rem(i, 3), lax.rem(i + 1, 3)
        if not last:
            @pl.when(i + 2 < count)
            def _():
                fill(i + 2, lax.rem(i + 2, 3))

        @pl.when(i >= 2)
        def _():
            result(i - 2).wait()
        steps = [weigh(i, slot, u, sc.at[par, u], top.at[par, u]) for u in range(2)]
        if not last:
            filled(i + 1, ahead)
            steps += [scores(ahead, u, sc.at[1 - par, u], top.at[1 - par, u]) for u in range(2)]
        both(*steps)
        result(i).start()

    fill(0, 0)
    if count > 1:
        fill(1, 1)
    filled(0, 0)
    both(*[scores(0, u, sc.at[0, u], top.at[0, u]) for u in range(2)])

    def pair(p, _):
        head(2 * p, 0, False)
        head(2 * p + 1, 1, False)
        return 0
    lax.fori_loop(0, (count - 1) // 2, pair, 0)
    if count % 2 == 0:
        head(jnp.int32(count - 2), 0, False)
    head(jnp.int32(count - 1), (count - 1) % 2, True)
    for i in range(max(0, count - 2), count):
        result(i).wait()


def attend(name, parts, *, s, place, q, state=None, gate=None):
    arrays, phases = {}, []
    for phase, columns, halos in parts:
        phases.append((phase, len(columns)))
        for c, (far, near) in enumerate(columns):
            arrays[f"F{phase}{c}"], arrays[f"N{phase}{c}"] = far, near
        arrays[f"E{phase}"], arrays[f"M{phase}"] = halos
    arrays.update(state=state, gate=gate)
    arrays = {n: x for n, x in arrays.items() if x is not None}
    names = tuple(arrays)
    heads = q.shape[3] // HD
    plan = (names, state is None, gate is not None, phases)
    shape = jax.ShapeDtypeStruct((heads, 2, ROWS, 2 * HD), jnp.float32)
    if gate is not None:
        shape = jax.ShapeDtypeStruct(q.shape, q.dtype)
    blocks = 3 * len(phases)
    return pl.pallas_call(
        functools.partial(attn_kernel, plan, 0, heads),
        out_shape=shape,
        in_specs=[SMEM, SMEM, ANY] + [VMEM if n == "gate" else ANY for n in names],
        out_specs=ANY,
        scratch_shapes=[
            pltpu.VMEM((3, 2, 2 * blocks, ROWS, HD), jnp.bfloat16),
            pltpu.VMEM((3, 12, 8, 8, HD), jnp.bfloat16),
            pltpu.VMEM((2, 2, ROWS, blocks * ROWS), jnp.float32),
            pltpu.VMEM((2, 2, ROWS, HD), jnp.float32),
            pltpu.VMEM((3, 2, ROWS, 2 * HD), jnp.float32),
            pltpu.VMEM((2, 2, ROWS, 2 * HD), jnp.float32),
            pltpu.VMEM((2, 12, 8, 8, HD), jnp.bfloat16),
            pltpu.SemaphoreType.DMA((3, 2)), pltpu.SemaphoreType.DMA((3,)),
            pltpu.SemaphoreType.DMA((3,)), pltpu.SemaphoreType.DMA((2,))],
        compiler_params=pltpu.CompilerParams(vmem_limit_bytes=60 * 2**20),
        cost_estimate=SMALL,
        name=name,
    )(s, place, q, *arrays.values())


def from_behind(block, distance):
    size = lax.axis_size("lon")
    return lax.ppermute(block, "lon", [((i - distance) % size, i) for i in range(size)])


def pairs(off):
    size = lax.axis_size("tm")
    return [[i + off, (i + off + 1) % size] for i in range(0, size, 2)]


def far_swap(x):
    route = [r for a, b in pairs(1)[:-1] for r in ((a, b), (b, a))]
    return lax.ppermute(x, "tm", route)


def near_swap(x):
    route = [r for a, b in pairs(0) for r in ((a, b), (b, a))]
    return lax.ppermute(x, "tm", route)


def local(query_field, key_field, value_field, tile_offsets, timesteps, gate_weight):
    heads = query_field.shape[3] // HD
    tiles = query_field.shape[0] // TT
    tm, size = lax.axis_index("tm"), lax.axis_size("tm")
    core = tm % 2
    cut = ((tm == 0) | (tm == size - 1)).astype(jnp.int32)
    shifts = tile_offsets[:, 0]
    mine = jnp.where(core == 0, shifts, shifts[::-1])
    place = jnp.stack([core, cut, far_swap(mine[:1])[0], near_swap(mine[1:])[0]])

    at = jnp.stack([core])
    xf = split("split_far", True, at, key_field, value_field)
    rf, lf = from_behind(xf, 1), from_behind(xf, -1)
    xn = split("split_near", False, at, key_field, value_field)
    rn, ln = from_behind(xn, 1), from_behind(xn, -1)
    r2f, l2f = from_behind(rf, 1), from_behind(lf, -1)
    r2n, l2n = from_behind(rn, 1), from_behind(ln, -1)

    half_freq = FREQ // 2
    frequencies = jnp.exp(-math.log(10000.0) * jnp.arange(half_freq, dtype=jnp.float32) / half_freq)
    angles = timesteps.astype(jnp.float32)[:, None] * frequencies[None, :]
    embedding = jnp.concatenate([jnp.cos(angles), jnp.sin(angles)], axis=1)
    gate_rows = jnp.dot(
        embedding, gate_weight, precision=lax.Precision.HIGHEST, preferred_element_type=jnp.float32
    ).reshape(tiles, heads, HD)

    attn = functools.partial(attend, s=tile_offsets, place=place, q=query_field)
    far0, near0 = far_swap(xf), near_swap(xn)
    later = hand_on(place, near0)
    far1 = far_swap(choose("far1", 1, 2, later, [rf, lf]))
    near1 = near_swap(choose("near1", 1, 3, later, [rn, ln]))
    far2 = choose("far2", 2, 2, hand_on(place, far0), [r2f, l2f, lf])
    far1, far2, gate_rows = lax.optimization_barrier((far1, far2, gate_rows))
    parts = [(0, [(xf, xn)], (far0, near0)), (1, [(rf, rn), (lf, ln)], (far1, near1))]
    state = attn("first", parts)

    r2n_, l2n_, state = lax.optimization_barrier((r2n, l2n, state))
    near2, far2 = lax.optimization_barrier((choose("near2", 2, 3, place, [r2n_, l2n_, ln]), far_swap(far2)))
    parts = [(2, [(r2f, r2n), (l2f, l2n), (lf, ln)], (far2, near_swap(near2)))]
    return attn("last", parts, state=state, gate=gate_rows)


def solution(mesh):
    return jax.shard_map(
        local,
        mesh=mesh,
        in_specs=(
            P("tm", None, "lon", "head"),
            P("tm", None, "lon", "head"),
            P("tm", None, "lon", "head"),
            P("tm", "lon"),
            P("tm"),
            P(None, "head"),
        ),
        out_specs=P("tm", None, "lon", "head"),
        check_vma=False,
    )
```

```python
import functools
import itertools
import math

import jax
import jax.numpy as jnp
from jax import lax
from jax.experimental import pallas as pl
from jax.experimental.pallas import tpu as pltpu
from jax.sharding import PartitionSpec as P

HD = 128
FREQ = 256
ROWS = 384
TT = 6
SCALE = math.log2(math.e) / math.sqrt(HD)
ANY = pl.BlockSpec(memory_space=pltpu.HBM)
SMALL = pl.CostEstimate(flops=0, bytes_accessed=1024, transcendentals=0)
VMEM = pl.BlockSpec(memory_space=pltpu.VMEM)
SMEM = pl.BlockSpec(memory_space=pltpu.SMEM)


PICKS = (lambda s: 0 * s, lambda s: jnp.where(s > 0, 1, 0), lambda s: jnp.where(s == 0, 2, jnp.where(s > 0, 1, 0)))


def split_kernel(far, place_ref, k_ref, v_ref, out, hold, into, out_of):
    core = place_ref[0]
    first = (core if far else 1 - core) * TT
    count = out.shape[0]
    last = []
    for i in range(count):
        for which, ref in enumerate((k_ref, v_ref)):
            source = ref.at[pl.ds(first, TT), :, :, pl.ds(i * HD, HD)]
            pltpu.make_async_copy(source, hold.at[i, which], into.at[i]).start()
        last.append(pltpu.make_async_copy(hold.at[i], out.at[i], out_of.at[i]))
    for i, copy in enumerate(last):
        pltpu.make_async_copy(hold.at[i], hold.at[i], into.at[i]).wait()
        copy.start()
    for copy in last:
        copy.wait()


def split(name, far, place, k, v):
    n = k.shape[3] // HD
    x = pl.pallas_call(
        functools.partial(split_kernel, far),
        out_shape=jax.ShapeDtypeStruct((n, 2, TT, 8, 8, HD), k.dtype),
        in_specs=[SMEM, ANY, ANY],
        out_specs=ANY,
        scratch_shapes=[pltpu.VMEM((n, 2, TT, 8, 8, HD), k.dtype), pltpu.SemaphoreType.DMA((n,)), pltpu.SemaphoreType.DMA((n,))],
        cost_estimate=SMALL,
        compiler_params=pltpu.CompilerParams(vmem_limit_bytes=60 * 2**20),
        name=name,
    )(place, k, v)
    return x.reshape(n, 2, ROWS, HD)


def hand_on_kernel(x_ref, *refs):
    out = refs[-1]
    for i in range(out.shape[0]):
        out[i] = x_ref[i]


def hand_on(x, *others):
    return pl.pallas_call(
        hand_on_kernel,
        out_shape=jax.ShapeDtypeStruct(x.shape, x.dtype),
        in_specs=[SMEM] + [ANY] * len(others),
        out_specs=SMEM,
        cost_estimate=SMALL,
        compiler_params=pltpu.CompilerParams(vmem_limit_bytes=60 * 2**20),
        name="hand_on",
    )(x, *others)


def choose_kernel(pick, slot, place_ref, *refs):
    ins, (out, hold, into, out_of) = refs[:-4], refs[-4:]
    side = pick(place_ref[slot])
    count = out.shape[0]
    for c, ref in enumerate(ins):
        @pl.when(side == c)
        def _():
            for i in range(count):
                pltpu.make_async_copy(ref.at[i], hold.at[i], into.at[i]).start()
    last = [pltpu.make_async_copy(hold.at[i], out.at[i], out_of.at[i]) for i in range(count)]
    for i, copy in enumerate(last):
        pltpu.make_async_copy(hold.at[i], hold.at[i], into.at[i]).wait()
        copy.start()
    for copy in last:
        copy.wait()


def choose(name, phase, slot, place, xs):
    x = xs[0]
    return pl.pallas_call(
        functools.partial(choose_kernel, PICKS[phase], slot),
        out_shape=jax.ShapeDtypeStruct(x.shape, x.dtype),
        in_specs=[SMEM] + [ANY] * len(xs),
        out_specs=ANY,
        scratch_shapes=[pltpu.VMEM(x.shape, x.dtype), pltpu.SemaphoreType.DMA(x.shape[:1]), pltpu.SemaphoreType.DMA(x.shape[:1])],
        cost_estimate=SMALL,
        compiler_params=pltpu.CompilerParams(vmem_limit_bytes=60 * 2**20),
        name=name,
    )(place, *xs)


def attn_kernel(plan, first, count, s_ref, place_ref, q_ref, *refs):
    names, starts, finishes, phases, units = plan
    blocks = [[(phase, b) for phase in phases for b in letters] for letters in ("EFN", "FNM")]
    ops = dict(zip(names, refs))
    out_ref, kv, qv, sc, top, si, so, ov, ksem, qsem, isem, osem = refs[len(refs) - 12:]
    core, cut = place_ref[0], place_ref[1]
    tiles = (core, 1 - core)
    width = [len(b) * ROWS for b in blocks]
    base = (0, len(blocks[0]))

    def fill(i, slot):
        h = first + i
        for u in units:
            for j, ((phase, sides), block) in enumerate(blocks[u]):
                side = PICKS[phase](s_ref[tiles[u], 0])
                to = kv.at[slot, :, base[u] + j]
                sem = ksem.at[slot, u]
                if block == "M":
                    pltpu.make_async_copy(ops[f"M{phase}"].at[h], to, sem).start()
                    continue
                if block == "E":
                    @pl.when(cut == 0)
                    def _():
                        pltpu.make_async_copy(ops[f"E{phase}"].at[h], to, sem).start()
                for c in range(sides):
                    name = f"{'N' if block == 'N' else 'F'}{phase}{c}"

                    @pl.when((side == c) & ((cut != 0) if block == "E" else True))
                    def _():
                        pltpu.make_async_copy(ops[name].at[h], to, sem).start()
        q_copy(i, slot).start()
        if not starts:
            state_in(i, slot).start()

    def filled(i, slot):
        for u in units:
            whole = kv.at[slot, :, pl.ds(base[u], len(blocks[u]))]
            pltpu.make_async_copy(whole, whole, ksem.at[slot, u]).wait()
        q_copy(i, slot).wait()
        if not starts:
            state_in(i, slot).wait()

    def lanes(i):
        return pl.ds(pl.multiple_of((first + i) * HD, HD), HD)

    def q_copy(i, slot):
        return pltpu.make_async_copy(q_ref.at[:, :, :, lanes(i)], qv.at[slot], qsem.at[slot])

    def state_in(i, slot):
        if len(units) == 1:
            return pltpu.make_async_copy(ops["state"].at[first + i, units[0]], si.at[slot, units[0]], isem.at[slot])
        return pltpu.make_async_copy(ops["state"].at[first + i], si.at[slot], isem.at[slot])

    def result(i):
        slot = lax.rem(i, 2)
        if len(units) == 1:
            frames = pl.ds(tiles[units[0]] * TT, TT)
            return pltpu.make_async_copy(ov.at[slot, frames], out_ref.at[frames, :, :, lanes(i)], osem.at[slot])
        if finishes:
            return pltpu.make_async_copy(ov.at[slot], out_ref.at[:, :, :, lanes(i)], osem.at[slot])
        return pltpu.make_async_copy(so.at[slot], out_ref.at[first + i], osem.at[slot])

    def stacked(slot, which, u):
        return kv[slot, which, base[u]:base[u] + len(blocks[u])].reshape(width[u], HD)

    def scores(slot, u, sc, top):
        k = stacked(slot, 0, u)
        step = ROWS
        for r in range(0, ROWS, step):
            q = qv[slot, pl.ds(tiles[u] * TT + r // 64, step // 64)].reshape(step, HD)
            s = lax.dot_general(q, k, (((1,), (1,)), ((), ())), preferred_element_type=jnp.float32)
            sc[r:r + step, :width[u]] = s
            m = s[:, :HD]
            for c in range(HD, width[u], HD):
                m = jnp.maximum(m, s[:, c:c + HD])
            m = jnp.broadcast_to(jnp.max(m, axis=1, keepdims=True), (step, HD))
            if not starts:
                m = jnp.maximum(m, jnp.broadcast_to(si[slot, u, r:r + step, HD:HD + 1], (step, HD)))
            top[r:r + step] = m
            yield

    def weigh(i, slot, u, sc, top):
        to = lax.rem(i, 2)
        v2 = []
        for j, (_, block) in enumerate(blocks[u]):
            v = jnp.concatenate([kv[slot, 1, base[u] + j], jnp.ones((ROWS, HD), jnp.bfloat16)], axis=1)
            v2.append(jnp.where(cut != 0, jnp.zeros_like(v), v) if block == "E" else v)
        v2 = jnp.concatenate(v2, axis=0)
        step = ROWS
        for r in range(0, ROWS, step):
            m1 = top[r:r + step]
            m = jnp.concatenate([m1] * (width[u] // HD), axis=1)
            p = jnp.exp2((sc[r:r + step, :width[u]] - m) * SCALE).astype(jnp.bfloat16)
            acc = jnp.dot(p, v2, preferred_element_type=jnp.float32)
            if not starts:
                old = si[slot, u, r:r + step, HD:]
                fade = jnp.exp2((jnp.broadcast_to(old[:, :1], (step, HD)) - m1) * SCALE)
                total = jnp.broadcast_to(old[:, HD - 1:], (step, HD))
                acc += jnp.concatenate([si[slot, u, r:r + step, :HD], total], axis=1) * jnp.concatenate([fade, fade], axis=1)
            if finishes:
                o = acc[:, :HD] / acc[:, HD:] * ops["gate"][tiles[u], first + i]
                ov[to, pl.ds(tiles[u] * TT + r // 64, step // 64)] = o.astype(jnp.bfloat16).reshape(step // 64, 8, 8, HD)
            else:
                lane = lax.broadcasted_iota(jnp.int32, (step, HD), 1)
                so[to, u, r:r + step, :HD] = acc[:, :HD]
                so[to, u, r:r + step, HD:] = jnp.where(lane < HD // 2, m1, acc[:, HD:])
            yield

    def both(*steps):
        for _ in itertools.zip_longest(*steps):
            pass

    def head(i, par, last):
        slot, ahead = lax.rem(i, 3), lax.rem(i + 1, 3)
        if not last:
            @pl.when(i + 2 < count)
            def _():
                fill(i + 2, lax.rem(i + 2, 3))

        @pl.when(i >= 2)
        def _():
            result(i - 2).wait()
        steps = [weigh(i, slot, u, sc.at[par, u], top.at[par, u]) for u in units]
        if not last:
            filled(i + 1, ahead)
            steps += [scores(ahead, u, sc.at[1 - par, u], top.at[1 - par, u]) for u in units]
        both(*steps)
        result(i).start()

    fill(0, 0)
    if count > 1:
        fill(1, 1)
    filled(0, 0)
    both(*[scores(0, u, sc.at[0, u], top.at[0, u]) for u in units])

    def pair(p, _):
        head(2 * p, 0, False)
        head(2 * p + 1, 1, False)
        return 0
    lax.fori_loop(0, (count - 1) // 2, pair, 0)
    if count % 2 == 0:
        head(jnp.int32(count - 2), 0, False)
    head(jnp.int32(count - 1), (count - 1) % 2, True)
    for i in range(max(0, count - 2), count):
        result(i).wait()


def attend(name, parts, *, s, place, q, units=(0, 1), state=None, gate=None, prev=None):
    arrays, phases = {}, []
    for phase, columns, halos in parts:
        phases.append((phase, len(columns)))
        for c, (far, near) in enumerate(columns):
            arrays[f"F{phase}{c}"], arrays[f"N{phase}{c}"] = far, near
        arrays[f"E{phase}"], arrays[f"M{phase}"] = halos
    arrays.update(state=state, gate=gate, prev=prev)
    arrays = {n: x for n, x in arrays.items() if x is not None}
    names = tuple(arrays)
    heads = q.shape[3] // HD
    plan = (names, state is None, gate is not None, phases, units)
    shape = jax.ShapeDtypeStruct((heads, 2, ROWS, 2 * HD), jnp.float32)
    if gate is not None:
        shape = jax.ShapeDtypeStruct(q.shape, q.dtype)
    blocks = 3 * len(phases)
    return pl.pallas_call(
        functools.partial(attn_kernel, plan, 0, heads),
        out_shape=shape,
        in_specs=[SMEM, SMEM, ANY] + [VMEM if n == "gate" else ANY for n in names],
        out_specs=ANY,
        input_output_aliases={} if prev is None else {3 + names.index("prev"): 0},
        scratch_shapes=[
            pltpu.VMEM((3, 2, 2 * blocks, ROWS, HD), jnp.bfloat16),
            pltpu.VMEM((3, 12, 8, 8, HD), jnp.bfloat16),
            pltpu.VMEM((2, 2, ROWS, blocks * ROWS), jnp.float32),
            pltpu.VMEM((2, 2, ROWS, HD), jnp.float32),
            pltpu.VMEM((3, 2, ROWS, 2 * HD), jnp.float32),
            pltpu.VMEM((2, 2, ROWS, 2 * HD), jnp.float32),
            pltpu.VMEM((2, 12, 8, 8, HD), jnp.bfloat16),
            pltpu.SemaphoreType.DMA((3, 2)), pltpu.SemaphoreType.DMA((3,)),
            pltpu.SemaphoreType.DMA((3,)), pltpu.SemaphoreType.DMA((2,))],
        compiler_params=pltpu.CompilerParams(vmem_limit_bytes=60 * 2**20),
        cost_estimate=SMALL,
        name=name,
    )(s, place, q, *arrays.values())


def from_behind(block, distance):
    size = lax.axis_size("lon")
    return lax.ppermute(block, "lon", [((i - distance) % size, i) for i in range(size)])


def pairs(off):
    size = lax.axis_size("tm")
    return [[i + off, (i + off + 1) % size] for i in range(0, size, 2)]


def far_swap(x):
    route = [r for a, b in pairs(1)[:-1] for r in ((a, b), (b, a))]
    return lax.ppermute(x, "tm", route)


def near_swap(x):
    route = [r for a, b in pairs(0) for r in ((a, b), (b, a))]
    return lax.ppermute(x, "tm", route)


def local(query_field, key_field, value_field, tile_offsets, timesteps, gate_weight):
    heads = query_field.shape[3] // HD
    tiles = query_field.shape[0] // TT
    tm, size = lax.axis_index("tm"), lax.axis_size("tm")
    core = tm % 2
    cut = ((tm == 0) | (tm == size - 1)).astype(jnp.int32)
    shifts = tile_offsets[:, 0]
    mine = jnp.where(core == 0, shifts, shifts[::-1])
    place = jnp.stack([core, cut, far_swap(mine[:1])[0], near_swap(mine[1:])[0]])

    at = jnp.stack([core])
    xf = split("split_far", True, at, key_field, value_field)
    rf, lf = from_behind(xf, 1), from_behind(xf, -1)
    xn = split("split_near", False, at, key_field, value_field)
    rn, ln = from_behind(xn, 1), from_behind(xn, -1)
    r2f, l2f = from_behind(rf, 1), from_behind(lf, -1)
    r2n, l2n = from_behind(rn, 1), from_behind(ln, -1)

    half_freq = FREQ // 2
    frequencies = jnp.exp(-math.log(10000.0) * jnp.arange(half_freq, dtype=jnp.float32) / half_freq)
    angles = timesteps.astype(jnp.float32)[:, None] * frequencies[None, :]
    embedding = jnp.concatenate([jnp.cos(angles), jnp.sin(angles)], axis=1)
    gate_rows = jnp.dot(
        embedding, gate_weight, precision=lax.Precision.HIGHEST, preferred_element_type=jnp.float32
    ).reshape(tiles, heads, HD)

    attn = functools.partial(attend, s=tile_offsets, place=place, q=query_field)
    far0, near0 = far_swap(xf), near_swap(xn)
    later = hand_on(place, near0)
    far1 = far_swap(choose("far1", 1, 2, later, [rf, lf]))
    near1 = near_swap(choose("near1", 1, 3, later, [rn, ln]))
    far2 = choose("far2", 2, 2, hand_on(place, far0), [r2f, l2f, lf])
    far1, far2, gate_rows = lax.optimization_barrier((far1, far2, gate_rows))
    parts = [(0, [(xf, xn)], (far0, near0)), (1, [(rf, rn), (lf, ln)], (far1, near1))]
    state = attn("first", parts)

    r2n_, l2n_, state = lax.optimization_barrier((r2n, l2n, state))
    near2, far2 = lax.optimization_barrier((choose("near2", 2, 3, place, [r2n_, l2n_, ln]), far_swap(far2)))
    columns = [(r2f, r2n), (l2f, l2n), (lf, ln)]
    near2 = near_swap(near2)
    out = attn("last_far", [(2, columns, (far2, None))], units=(0,), state=state, gate=gate_rows)
    return attn("last_near", [(2, columns, (None, near2))], units=(1,), state=state, gate=gate_rows, prev=out)


def solution(mesh):
    return jax.shard_map(
        local,
        mesh=mesh,
        in_specs=(
            P("tm", None, "lon", "head"),
            P("tm", None, "lon", "head"),
            P("tm", None, "lon", "head"),
            P("tm", "lon"),
            P("tm"),
            P(None, "head"),
        ),
        out_specs=P("tm", None, "lon", "head"),
        check_vma=False,
    )
```

```python
import functools
import itertools
import math

import jax
import jax.numpy as jnp
from jax import lax
from jax.experimental import pallas as pl
from jax.experimental.pallas import tpu as pltpu
from jax.sharding import PartitionSpec as P

HD = 128
FREQ = 256
ROWS = 384
TT = 6
SCALE = math.log2(math.e) / math.sqrt(HD)
ANY = pl.BlockSpec(memory_space=pltpu.HBM)
SMALL = pl.CostEstimate(flops=0, bytes_accessed=1024, transcendentals=0)
VMEM = pl.BlockSpec(memory_space=pltpu.VMEM)
SMEM = pl.BlockSpec(memory_space=pltpu.SMEM)


PICKS = (lambda s: 0 * s, lambda s: jnp.where(s > 0, 1, 0), lambda s: jnp.where(s == 0, 2, jnp.where(s > 0, 1, 0)))


def split_kernel(far, place_ref, k_ref, v_ref, out, hold, into, out_of):
    core = place_ref[0]
    first = (core if far else 1 - core) * TT
    count = out.shape[0]
    last = []
    for i in range(count):
        for which, ref in enumerate((k_ref, v_ref)):
            source = ref.at[pl.ds(first, TT), :, :, pl.ds(i * HD, HD)]
            pltpu.make_async_copy(source, hold.at[i, which], into.at[i]).start()
        last.append(pltpu.make_async_copy(hold.at[i], out.at[i], out_of.at[i]))
    for i, copy in enumerate(last):
        pltpu.make_async_copy(hold.at[i], hold.at[i], into.at[i]).wait()
        copy.start()
    for copy in last:
        copy.wait()


def split(name, far, place, k, v):
    n = k.shape[3] // HD
    x = pl.pallas_call(
        functools.partial(split_kernel, far),
        out_shape=jax.ShapeDtypeStruct((n, 2, TT, 8, 8, HD), k.dtype),
        in_specs=[SMEM, ANY, ANY],
        out_specs=ANY,
        scratch_shapes=[pltpu.VMEM((n, 2, TT, 8, 8, HD), k.dtype), pltpu.SemaphoreType.DMA((n,)), pltpu.SemaphoreType.DMA((n,))],
        cost_estimate=SMALL,
        compiler_params=pltpu.CompilerParams(vmem_limit_bytes=60 * 2**20),
        name=name,
    )(place, k, v)
    return x.reshape(n, 2, ROWS, HD)


def hand_on_kernel(x_ref, *refs):
    out = refs[-1]
    for i in range(out.shape[0]):
        out[i] = x_ref[i]


def hand_on(x, *others):
    return pl.pallas_call(
        hand_on_kernel,
        out_shape=jax.ShapeDtypeStruct(x.shape, x.dtype),
        in_specs=[SMEM] + [ANY] * len(others),
        out_specs=SMEM,
        cost_estimate=SMALL,
        compiler_params=pltpu.CompilerParams(vmem_limit_bytes=60 * 2**20),
        name="hand_on",
    )(x, *others)


def choose_kernel(pick, slot, place_ref, *refs):
    ins, (out, hold, into, out_of) = refs[:-4], refs[-4:]
    side = pick(place_ref[slot])
    count = out.shape[0]
    for c, ref in enumerate(ins):
        @pl.when(side == c)
        def _():
            for i in range(count):
                pltpu.make_async_copy(ref.at[i], hold.at[i], into.at[i]).start()
    last = [pltpu.make_async_copy(hold.at[i], out.at[i], out_of.at[i]) for i in range(count)]
    for i, copy in enumerate(last):
        pltpu.make_async_copy(hold.at[i], hold.at[i], into.at[i]).wait()
        copy.start()
    for copy in last:
        copy.wait()


def choose(name, phase, slot, place, xs):
    x = xs[0]
    return pl.pallas_call(
        functools.partial(choose_kernel, PICKS[phase], slot),
        out_shape=jax.ShapeDtypeStruct(x.shape, x.dtype),
        in_specs=[SMEM] + [ANY] * len(xs),
        out_specs=ANY,
        scratch_shapes=[pltpu.VMEM(x.shape, x.dtype), pltpu.SemaphoreType.DMA(x.shape[:1]), pltpu.SemaphoreType.DMA(x.shape[:1])],
        cost_estimate=SMALL,
        compiler_params=pltpu.CompilerParams(vmem_limit_bytes=60 * 2**20),
        name=name,
    )(place, *xs)


def attn_kernel(plan, first, count, s_ref, place_ref, q_ref, *refs):
    names, starts, finishes, phases = plan
    blocks = [[(phase, b) for phase in phases for b in letters] for letters in ("EFN", "FNM")]
    ops = dict(zip(names, refs))
    out_ref, kv, qv, sc, top, si, so, ov, ksem, qsem, isem, osem = refs[len(refs) - 12:]
    core, cut = place_ref[0], place_ref[1]
    tiles = (core, 1 - core)
    width = [len(b) * ROWS for b in blocks]
    base = (0, len(blocks[0]))

    def fill(i, slot):
        h = first + i
        for u in range(2):
            for j, ((phase, sides), block) in enumerate(blocks[u]):
                side = PICKS[phase](s_ref[tiles[u], 0])
                to = kv.at[slot, :, base[u] + j]
                sem = ksem.at[slot, u]
                if block == "M":
                    pltpu.make_async_copy(ops[f"M{phase}"].at[h], to, sem).start()
                    continue
                if block == "E":
                    @pl.when(cut == 0)
                    def _():
                        pltpu.make_async_copy(ops[f"E{phase}"].at[h], to, sem).start()
                for c in range(sides):
                    name = f"{'N' if block == 'N' else 'F'}{phase}{c}"

                    @pl.when((side == c) & ((cut != 0) if block == "E" else True))
                    def _():
                        pltpu.make_async_copy(ops[name].at[h], to, sem).start()
        q_copy(i, slot).start()
        if not starts:
            state_in(i, slot).start()

    def filled(i, slot):
        for u in range(2):
            whole = kv.at[slot, :, pl.ds(base[u], len(blocks[u]))]
            pltpu.make_async_copy(whole, whole, ksem.at[slot, u]).wait()
        q_copy(i, slot).wait()
        if not starts:
            state_in(i, slot).wait()

    def lanes(i):
        return pl.ds(pl.multiple_of((first + i) * HD, HD), HD)

    def q_copy(i, slot):
        return pltpu.make_async_copy(q_ref.at[:, :, :, lanes(i)], qv.at[slot], qsem.at[slot])

    def state_in(i, slot):
        return pltpu.make_async_copy(ops["state"].at[first + i], si.at[slot], isem.at[slot])

    def result(i):
        slot = lax.rem(i, 2)
        if finishes:
            return pltpu.make_async_copy(ov.at[slot], out_ref.at[:, :, :, lanes(i)], osem.at[slot])
        return pltpu.make_async_copy(so.at[slot], out_ref.at[first + i], osem.at[slot])

    def stacked(slot, which, u):
        return kv[slot, which, base[u]:base[u] + len(blocks[u])].reshape(width[u], HD)

    def scores(slot, u, sc, top):
        k = stacked(slot, 0, u)
        step = ROWS
        for r in range(0, ROWS, step):
            q = qv[slot, pl.ds(tiles[u] * TT + r // 64, step // 64)].reshape(step, HD)
            s = lax.dot_general(q, k, (((1,), (1,)), ((), ())), preferred_element_type=jnp.float32)
            sc[r:r + step, :width[u]] = s
            m = s[:, :HD]
            for c in range(HD, width[u], HD):
                m = jnp.maximum(m, s[:, c:c + HD])
            m = jnp.broadcast_to(jnp.max(m, axis=1, keepdims=True), (step, HD))
            if not starts:
                m = jnp.maximum(m, jnp.broadcast_to(si[slot, u, r:r + step, HD:HD + 1], (step, HD)))
            top[r:r + step] = m
            yield

    def weigh(i, slot, u, sc, top):
        to = lax.rem(i, 2)
        v2 = []
        for j, (_, block) in enumerate(blocks[u]):
            v = jnp.concatenate([kv[slot, 1, base[u] + j], jnp.ones((ROWS, HD), jnp.bfloat16)], axis=1)
            v2.append(jnp.where(cut != 0, jnp.zeros_like(v), v) if block == "E" else v)
        v2 = jnp.concatenate(v2, axis=0)
        step = ROWS
        for r in range(0, ROWS, step):
            m1 = top[r:r + step]
            m = jnp.concatenate([m1] * (width[u] // HD), axis=1)
            p = jnp.exp2((sc[r:r + step, :width[u]] - m) * SCALE).astype(jnp.bfloat16)
            acc = jnp.dot(p, v2, preferred_element_type=jnp.float32)
            if not starts:
                old = si[slot, u, r:r + step, HD:]
                fade = jnp.exp2((jnp.broadcast_to(old[:, :1], (step, HD)) - m1) * SCALE)
                total = jnp.broadcast_to(old[:, HD - 1:], (step, HD))
                acc += jnp.concatenate([si[slot, u, r:r + step, :HD], total], axis=1) * jnp.concatenate([fade, fade], axis=1)
            if finishes:
                o = acc[:, :HD] / acc[:, HD:] * ops["gate"][tiles[u], first + i]
                ov[to, pl.ds(tiles[u] * TT + r // 64, step // 64)] = o.astype(jnp.bfloat16).reshape(step // 64, 8, 8, HD)
            else:
                lane = lax.broadcasted_iota(jnp.int32, (step, HD), 1)
                so[to, u, r:r + step, :HD] = acc[:, :HD]
                so[to, u, r:r + step, HD:] = jnp.where(lane < HD // 2, m1, acc[:, HD:])
            yield

    def both(*steps):
        for _ in itertools.zip_longest(*steps):
            pass

    def head(i, par):
        slot, ahead = lax.rem(i, 3), lax.rem(i + 1, 3)

        @pl.when(i + 2 < count)
        def _():
            fill(i + 2, lax.rem(i + 2, 3))

        @pl.when(i >= 2)
        def _():
            result(i - 2).wait()
        steps = [weigh(i, slot, u, sc.at[par, u], top.at[par, u]) for u in range(2)]

        @pl.when(i + 1 < count)
        def _():
            filled(i + 1, ahead)
        steps += [scores(ahead, u, sc.at[1 - par, u], top.at[1 - par, u]) for u in range(2)]
        both(*steps)
        result(i).start()

    fill(0, 0)
    if count > 1:
        fill(1, 1)
    filled(0, 0)
    both(*[scores(0, u, sc.at[0, u], top.at[0, u]) for u in range(2)])

    def pair(p, _):
        head(2 * p, 0)
        head(2 * p + 1, 1)
        return 0
    lax.fori_loop(0, count // 2, pair, 0)
    for i in range(max(0, count - 2), count):
        result(i).wait()


def attend(name, parts, *, s, place, q, state=None, gate=None):
    arrays, phases = {}, []
    for phase, columns, halos in parts:
        phases.append((phase, len(columns)))
        for c, (far, near) in enumerate(columns):
            arrays[f"F{phase}{c}"], arrays[f"N{phase}{c}"] = far, near
        arrays[f"E{phase}"], arrays[f"M{phase}"] = halos
    arrays.update(state=state, gate=gate)
    arrays = {n: x for n, x in arrays.items() if x is not None}
    names = tuple(arrays)
    heads = q.shape[3] // HD
    plan = (names, state is None, gate is not None, phases)
    shape = jax.ShapeDtypeStruct((heads, 2, ROWS, 2 * HD), jnp.float32)
    if gate is not None:
        shape = jax.ShapeDtypeStruct(q.shape, q.dtype)
    blocks = 3 * len(phases)
    return pl.pallas_call(
        functools.partial(attn_kernel, plan, 0, heads),
        out_shape=shape,
        in_specs=[SMEM, SMEM, ANY] + [VMEM if n == "gate" else ANY for n in names],
        out_specs=ANY,
        scratch_shapes=[
            pltpu.VMEM((3, 2, 2 * blocks, ROWS, HD), jnp.bfloat16),
            pltpu.VMEM((3, 12, 8, 8, HD), jnp.bfloat16),
            pltpu.VMEM((2, 2, ROWS, blocks * ROWS), jnp.float32),
            pltpu.VMEM((2, 2, ROWS, HD), jnp.float32),
            pltpu.VMEM((3, 2, ROWS, 2 * HD), jnp.float32),
            pltpu.VMEM((2, 2, ROWS, 2 * HD), jnp.float32),
            pltpu.VMEM((2, 12, 8, 8, HD), jnp.bfloat16),
            pltpu.SemaphoreType.DMA((3, 2)), pltpu.SemaphoreType.DMA((3,)),
            pltpu.SemaphoreType.DMA((3,)), pltpu.SemaphoreType.DMA((2,))],
        compiler_params=pltpu.CompilerParams(vmem_limit_bytes=60 * 2**20),
        cost_estimate=SMALL,
        name=name,
    )(s, place, q, *arrays.values())


def from_behind(block, distance):
    size = lax.axis_size("lon")
    return lax.ppermute(block, "lon", [((i - distance) % size, i) for i in range(size)])


def pairs(off):
    size = lax.axis_size("tm")
    return [[i + off, (i + off + 1) % size] for i in range(0, size, 2)]


def far_swap(x):
    route = [r for a, b in pairs(1)[:-1] for r in ((a, b), (b, a))]
    return lax.ppermute(x, "tm", route)


def near_swap(x):
    route = [r for a, b in pairs(0) for r in ((a, b), (b, a))]
    return lax.ppermute(x, "tm", route)


def local(query_field, key_field, value_field, tile_offsets, timesteps, gate_weight):
    heads = query_field.shape[3] // HD
    tiles = query_field.shape[0] // TT
    tm, size = lax.axis_index("tm"), lax.axis_size("tm")
    core = tm % 2
    cut = ((tm == 0) | (tm == size - 1)).astype(jnp.int32)
    shifts = tile_offsets[:, 0]
    mine = jnp.where(core == 0, shifts, shifts[::-1])
    place = jnp.stack([core, cut, far_swap(mine[:1])[0], near_swap(mine[1:])[0]])

    at = jnp.stack([core])
    xf = split("split_far", True, at, key_field, value_field)
    rf, lf = from_behind(xf, 1), from_behind(xf, -1)
    xn = split("split_near", False, at, key_field, value_field)
    rn, ln = from_behind(xn, 1), from_behind(xn, -1)
    r2f, l2f = from_behind(rf, 1), from_behind(lf, -1)
    r2n, l2n = from_behind(rn, 1), from_behind(ln, -1)

    half_freq = FREQ // 2
    frequencies = jnp.exp(-math.log(10000.0) * jnp.arange(half_freq, dtype=jnp.float32) / half_freq)
    angles = timesteps.astype(jnp.float32)[:, None] * frequencies[None, :]
    embedding = jnp.concatenate([jnp.cos(angles), jnp.sin(angles)], axis=1)
    gate_rows = jnp.dot(
        embedding, gate_weight, precision=lax.Precision.HIGHEST, preferred_element_type=jnp.float32
    ).reshape(tiles, heads, HD)

    attn = functools.partial(attend, s=tile_offsets, place=place, q=query_field)
    far0, near0 = far_swap(xf), near_swap(xn)
    later = hand_on(place, near0)
    far1 = far_swap(choose("far1", 1, 2, later, [rf, lf]))
    near1 = near_swap(choose("near1", 1, 3, later, [rn, ln]))
    far2 = choose("far2", 2, 2, hand_on(place, far0), [r2f, l2f, lf])
    far1, far2, gate_rows = lax.optimization_barrier((far1, far2, gate_rows))
    parts = [(0, [(xf, xn)], (far0, near0)), (1, [(rf, rn), (lf, ln)], (far1, near1))]
    state = attn("first", parts)

    r2n_, l2n_, state = lax.optimization_barrier((r2n, l2n, state))
    near2, far2 = lax.optimization_barrier((choose("near2", 2, 3, place, [r2n_, l2n_, ln]), far_swap(far2)))
    parts = [(2, [(r2f, r2n), (l2f, l2n), (lf, ln)], (far2, near_swap(near2)))]
    return attn("last", parts, state=state, gate=gate_rows)


def solution(mesh):
    return jax.shard_map(
        local,
        mesh=mesh,
        in_specs=(
            P("tm", None, "lon", "head"),
            P("tm", None, "lon", "head"),
            P("tm", None, "lon", "head"),
            P("tm", "lon"),
            P("tm"),
            P(None, "head"),
        ),
        out_specs=P("tm", None, "lon", "head"),
        check_vma=False,
    )
```
